128 devices in a mesh: dp: 32 (over z_lo, y, x), mp: 4 (over z_hi, core).
Axes of the slice: x: 4, y: 4, z: 4 (z_hi: 2, z_lo: 2; z = z_hi * 2 + z_lo), core: 2. Of those that a mesh axis runs over, the one named last changes fastest.
Arguments:
- pooled: bfloat16 [10240, 1792], P('dp'), may hold values from -6 to 6
- ln_gain: float32 [1792], replicated, may hold values from 0.5 to 1.5
- w_in: bfloat16 [15360, 1792], P(('dp', 'mp')), may hold values from -0.125 to 0.125
- w_out: bfloat16 [15360, 1792], P(('dp', 'mp')), may hold values from -0.046875 to 0.046875
- proj: bfloat16 [1792, 1024], replicated, may hold values from -0.125 to 0.125
- text: bfloat16 [10240, 1024], P(('dp', 'mp')), may hold values from -6 to 6
- logit_scale: float32 [1], replicated, may hold values from 5 to 15
- logit_bias: float32 [1], replicated, may hold values from -1 to 1
Outputs:
- d_pooled: float32 [10240, 1792], P(('dp', 'mp'))
- proj_grad: float32 [1792, 1024], P('dp', 'mp')
- text_grad: float32 [10240, 1024], P(('dp', 'mp'))
The draws below stay inside these ranges and needn't reach their ends.
All inputs are finite; a program needn't handle non-finite values.
Results may differ from the reference program's by a relative error of at most 0.029.
Values may be sent and summed in bfloat16 or wider, within the bound.
A program may use at most 128 MiB of HBM per device.

```python
import jax
import jax.numpy as jnp
from jax import lax

D = 1792
FF = 15360
E = 1024
B_DEV = 320
STEPS = 4
BATCH = 10240
N_DP = 32


def strengthened(array, own_key, source, target, parts, factor):
    def block_of(dim):
        return (jnp.arange(array.shape[dim]) // (array.shape[dim] // parts)).reshape((-1,) + (1,) * (array.ndim - 1 - dim))

    first = jax.random.permutation(own_key, parts)[block_of(target)]
    second = (block_of(target) + parts // 2) % parts
    return jnp.where((block_of(source) == first) | (block_of(source) == second), factor * array, array)


def levels(key, dims, pieces, low, largest):
    def one(axis_at, shards_of):
        steps = jax.random.uniform(jax.random.fold_in(jax.random.fold_in(key, 6), axis_at), (shards_of,), jnp.float32, low / len(pieces), largest / len(pieces))
        return jnp.repeat(jnp.exp(steps), dims[axis_at] // shards_of).reshape((-1,) + (1,) * (len(dims) - axis_at - 1))

    loudness = one(*pieces[0])
    for cut in pieces[1:]:
        loudness = loudness * one(*cut)
    return loudness


def normal_values(own_key, dims, scale, limit, pieces=(), kind=jnp.bfloat16):
    entries = scale * jax.random.normal(own_key, dims, jnp.float32)
    if pieces:
        entries = entries * levels(own_key, dims, pieces, -0.22, 0.18)
    return jnp.clip(entries, -limit, limit).astype(kind)


def heavy_noise(own_key, extent, width, bound, pieces, heavy, dtype=jnp.bfloat16):
    array = width * jax.random.normal(own_key, extent, jnp.float32)
    if pieces:
        array = array * levels(own_key, extent, pieces, -0.22, 0.18)
    return jnp.clip(strengthened(array, jax.random.fold_in(own_key, 3), *heavy), -bound, bound).astype(dtype)


def setup_inputs(seed: int = 0) -> dict:
    key_list = jax.random.split(jax.random.key(seed), 9)
    pooled = heavy_noise(key_list[0], (BATCH, D), 1.0, 6.0, ((0, 32),), (0, 1, 32, 2.75))
    ln_gain = jnp.clip(1.0 + 0.1 * jax.random.normal(key_list[1], (D,), jnp.float32), 0.5, 1.5)
    w_in = normal_values(key_list[2], (FF, D), D ** -0.5, 0.125, ((0, 128),))
    w_out = normal_values(key_list[3], (FF, D), FF ** -0.5, 0.046875, ((0, 128),))
    proj = normal_values(key_list[4], (D, E), D ** -0.5, 0.125)
    text = normal_values(key_list[5], (BATCH, E), 1.0, 6.0, ((0, 128),))
    logit_scale = jnp.clip(jax.random.uniform(key_list[6], (1,), jnp.float32, 5.0, 15.0), 5.0, 15.0)
    logit_bias = jnp.clip(jax.random.uniform(key_list[7], (1,), jnp.float32, -1.0, 1.0), -1.0, 1.0)
    return dict(pooled=pooled, ln_gain=ln_gain, w_in=w_in, w_out=w_out, proj=proj, text=text, logit_scale=logit_scale, logit_bias=logit_bias)


def gelu_tanh(values):
    return jax.nn.gelu(values, approximate=True)

def norm_parts(hblock):
    hidden_f = hblock.astype(jnp.float32)
    center = hidden_f - lax.optimization_barrier(jnp.mean(hidden_f, axis=-1, keepdims=True))
    inv_std = lax.rsqrt(lax.optimization_barrier(jnp.mean(center * center, axis=-1, keepdims=True)) + 1e-06)
    return (center * inv_std, inv_std)

def block_forward(hblock, ln_gain, w_in, w_out):
    normed, inv_std = norm_parts(hblock)
    x_in = (normed * ln_gain).astype(jnp.bfloat16)
    hidden_pre = jnp.dot(x_in, w_in.T, preferred_element_type=jnp.float32)
    hidden_act = gelu_tanh(hidden_pre).astype(jnp.bfloat16)
    mixed = jnp.dot(hidden_act, w_out, preferred_element_type=jnp.float32)
    return hblock.astype(jnp.float32) + mixed

def block_backward(hblock, grad_bf, resid_grad, ln_gain, w_in, w_out):
    normed, inv_std = norm_parts(hblock)
    x_in = (normed * ln_gain).astype(jnp.bfloat16)
    hidden_pre = jnp.dot(x_in, w_in.T, preferred_element_type=jnp.float32)
    hidden_act, gelu_back = jax.vjp(gelu_tanh, hidden_pre)
    act_grad = jnp.dot(grad_bf, w_out.T, preferred_element_type=jnp.float32)
    pre_grad = gelu_back(act_grad)[0].astype(jnp.bfloat16)
    input_grad = jnp.dot(pre_grad, w_in, preferred_element_type=jnp.float32)
    scaled = input_grad * ln_gain
    shifted = scaled - lax.optimization_barrier(jnp.mean(scaled, axis=-1, keepdims=True))
    shifted = shifted - normed * lax.optimization_barrier(jnp.mean(scaled * normed, axis=-1, keepdims=True))
    return resid_grad + inv_std * shifted

def reference(pooled, ln_gain, w_in, w_out, proj, text, logit_scale, logit_bias):
    blocks_h = pooled.reshape(N_DP, B_DEV, D)
    resid = lax.map(lambda hb: block_forward(hb, ln_gain, w_in, w_out), blocks_h).reshape(BATCH, D)
    resid_bf = resid.astype(jnp.bfloat16)
    project = jnp.dot(resid_bf, proj, preferred_element_type=jnp.float32)
    inverse = lax.rsqrt(lax.optimization_barrier(jnp.sum(project * project, axis=-1, keepdims=True)) + 1e-06)
    embeds = (project * inverse).astype(jnp.bfloat16)
    text_f = text.astype(jnp.float32)
    text_inv = lax.rsqrt(lax.optimization_barrier(jnp.sum(text_f * text_f, axis=-1, keepdims=True)) + 1e-06)
    text_unit = (text_f * text_inv).astype(jnp.bfloat16)
    scaling = logit_scale[0]
    offset = logit_bias[0]
    embed_blocks = embeds.reshape(N_DP, B_DEV, E).astype(jnp.float32)
    unit_blocks = text_unit.reshape(N_DP, B_DEV, E).astype(jnp.float32)
    same_pair = jnp.arange(B_DEV)[:, None] == jnp.arange(B_DEV)[None, :]
    embed_grad = jnp.zeros((N_DP, B_DEV, E), jnp.float32)
    unit_grad = jnp.zeros((N_DP, B_DEV, E), jnp.float32)
    for step in range(STEPS):
        partner = jnp.roll(unit_blocks, step, axis=0)
        logits = scaling * jnp.einsum('imd,ind->imn', embed_blocks, partner) + offset
        if step == 0:
            label = jnp.where(same_pair, 1.0, -1.0).astype(jnp.float32)
        else:
            label = -jnp.ones((B_DEV, B_DEV), jnp.float32)
        coef = (-label * jax.nn.sigmoid(-label * logits)).astype(jnp.bfloat16).astype(jnp.float32)
        embed_grad = embed_grad + scaling * jnp.einsum('imn,ind->imd', coef, partner)
        term = scaling * jnp.einsum('imn,imd->ind', coef, embed_blocks)
        unit_grad = unit_grad + jnp.roll(term, -step, axis=0)
    unit_grad = unit_grad.reshape(BATCH, E)
    embed_grad = embed_grad.reshape(BATCH, E)
    text_unit_f = text_f * text_inv
    text_grad = text_inv * (unit_grad - text_unit_f * lax.optimization_barrier(jnp.sum(text_unit_f * unit_grad, axis=-1, keepdims=True)))
    unit_f = project * inverse
    proj_delta = (inverse * (embed_grad - unit_f * lax.optimization_barrier(jnp.sum(unit_f * embed_grad, axis=-1, keepdims=True)))).astype(jnp.bfloat16)
    proj_grad = jnp.dot(resid_bf.T, proj_delta, preferred_element_type=jnp.float32)
    resid_grad = jnp.dot(proj_delta, proj.T, preferred_element_type=jnp.float32)
    grad_bf = resid_grad.astype(jnp.bfloat16)
    d_pooled = lax.map(lambda args: block_backward(args[0], args[1], args[2], ln_gain, w_in, w_out), (blocks_h, grad_bf.reshape(N_DP, B_DEV, D), resid_grad.reshape(N_DP, B_DEV, D)))
    return (d_pooled.reshape(BATCH, D), proj_grad, text_grad)
```

```python
import functools

import jax
import jax.numpy as jnp
from jax import lax
from jax.experimental import pallas as pl
from jax.experimental.pallas import tpu as pltpu
from jax.sharding import PartitionSpec as P

D = 1792
H = D // 2
E = 1024
U = 120
R = 80
F32 = jnp.float32
BF16 = jnp.bfloat16
MESH = pl.DeviceIdType.MESH
PAIRS = (
    ((0, 0), (3, 0)),
    ((1, 0), (0, 3)),
    ((0, 1), (3, 3)),
    ((3, 1), (1, 3)),
    ((1, 1), (2, 0)),
    ((0, 2), (2, 3)),
    ((2, 1), (3, 2)),
    ((1, 2), (2, 2)),
)
N_SEMS = 128


def mm(a, b):
    return lax.dot_general(a, b, (((1,), (0,)), ((), ())), preferred_element_type=F32)


def mm_nt(a, b):
    return lax.dot_general(a, b, (((1,), (1,)), ((), ())), preferred_element_type=F32)


def mm_tn(a, b):
    return lax.dot_general(a, b, (((0,), (0,)), ((), ())), preferred_element_type=F32)


def gelu_and_slope(v):
    c = 0.7978845608028654
    v2 = v * v
    t = jnp.tanh(c * v * (1.0 + 0.044715 * v2))
    half = 0.5 * (1.0 + t)
    act = v * half
    slope = half + (0.5 * v) * (1.0 - t * t) * (c * (1.0 + 3.0 * 0.044715 * v2))
    return act, slope


def kernel(
    pooled, gain, w_in, w_out, proj_hbm, text, scale, bias,
    d_pooled, proj_grad, text_grad,
    slot_in, slot_out, dense_in, dense_out, x, acc, slope, grad_bf, resid_grad,
    tall, eall, proj, stage, core_in, hop, fin, direct, pd, resid_bf, rs, rs_hop,
    pg, pg_in, pg2, pg2_in, send_sems, recv_sems, local_sems,
):
    dp = lax.axis_index("dp")
    mp = lax.axis_index("mp")
    z_lo = dp // 16
    yi = (dp // 4) % 4
    xi = dp % 4
    z_hi = mp // 2
    c = mp % 2
    z = z_hi * 2 + z_lo

    def place(dx=0, dy=0, dz=0, other=False):
        nz = (z + dz) % 4
        ndp = (nz % 2) * 16 + ((yi + dy) % 4) * 4 + (xi + dx) % 4
        nmp = (nz // 2) * 2 + (1 - c if other else c)
        return {"dp": ndp, "mp": nmp}

    def shifted(k):
        return {"dp": (dp + k + 32) % 32, "mp": mp}

    x_fwd, x_bwd, x_far = place(dx=1), place(dx=3), place(dx=2)
    y_fwd, y_bwd, y_far = place(dy=1), place(dy=3), place(dy=2)
    z_fwd, z_bwd, z_far = place(dz=1), place(dz=3), place(dz=2)
    core = place(other=True)

    count = [0]
    started = []

    def send(src, dst, where):
        n = count[0]
        count[0] += 1
        copy = pltpu.make_async_remote_copy(
            src_ref=src, dst_ref=dst, send_sem=send_sems.at[n], recv_sem=recv_sems.at[n],
            device_id=where, device_id_type=MESH,
        )
        copy.start()
        started.append(copy)
        return copy

    def slot(dx, dy):
        return dy * 4 + dx

    locals_ = [
        pltpu.make_async_copy(w_in, slot_in.at[0], local_sems.at[0]),
        pltpu.make_async_copy(w_out, slot_out.at[0], local_sems.at[1]),
        pltpu.make_async_copy(proj_hbm, proj, local_sems.at[2]),
    ]
    for copy in locals_:
        copy.start()

    peers = [x_fwd, x_bwd, x_far, y_fwd, y_bwd, y_far, z_fwd, z_bwd, z_far, core]
    peers += [shifted(k) for k in (-3, -2, -1, 1, 2, 3)]
    barrier = pltpu.get_barrier_semaphore()
    for peer in peers:
        pl.semaphore_signal(barrier, inc=1, device_id=peer, device_id_type=MESH)
    pl.semaphore_wait(barrier, len(peers))

    arrive = {}

    def give(which, ref, src, dst_slot, where, half=None):
        if half is None:
            target = ref.at[dst_slot]
            source = src
        else:
            columns = pl.ds(half * H, H)
            target = ref.at[dst_slot, :, columns]
            source = src.at[:, columns]
        arrive[which, dst_slot, half] = send(source, target, where)

    A, B = ("in", slot_in), ("out", slot_out)
    give(*A, w_in, slot(3, 0), x_fwd)
    give(*A, w_in, slot(1, 0), x_bwd)
    give(*B, w_out, slot(0, 3), y_fwd)
    give(*B, w_out, slot(0, 1), y_bwd)
    give(*B, w_out, slot(3, 0), x_fwd)
    give(*B, w_out, slot(1, 0), x_bwd)
    give(*A, w_in, slot(0, 3), y_fwd)
    give(*A, w_in, slot(0, 1), y_bwd)

    def text_parts():
        t = text[...].astype(F32)
        inv = lax.rsqrt(jnp.sum(t * t, axis=-1, keepdims=True) + 1e-06)
        return t * inv, inv

    tall[0, 0] = text_parts()[0].astype(BF16)
    text_first = [send(tall.at[0, 0], tall.at[0, k], shifted(k)) for k in (1, 2, 3)]

    def norm_rows(start):
        h = pooled[pl.ds(pl.multiple_of(start, 16), R), :].astype(F32)
        center = h - jnp.mean(h, axis=-1, keepdims=True)
        inv_std = lax.rsqrt(jnp.mean(center * center, axis=-1, keepdims=True) + 1e-06)
        return h, center * inv_std, inv_std

    own_row = z_hi * 160 + c * R
    other_row = z_hi * 160 + (1 - c) * R
    far_own = (1 - z_hi) * 160 + c * R
    far_other = (1 - z_hi) * 160 + (1 - c) * R

    def fill_x(dz, j, start):
        x[dz, j * R:(j + 1) * R, :] = (norm_rows(start)[1] * gain[...]).astype(BF16)

    fill_x(0, 0, own_row)
    fill_x(0, 1, other_row)
    x_up = send(x.at[0], x.at[3], z_fwd)
    x_down = send(x.at[0], x.at[1], z_bwd)
    fill_x(2, 0, far_own)
    fill_x(2, 1, far_other)

    def got(which, where, half=None):
        arrive[which, slot(*where), half].wait_recv()

    def spread(which, ref, where, axis, half_also=True):
        dx, dy = where
        src = ref.at[slot(dx, dy)]
        if axis == "y":
            give(which, ref, src, slot(dx, 3), y_fwd)
            give(which, ref, src, slot(dx, 1), y_bwd)
        else:
            give(which, ref, src, slot(3, dy), x_fwd)
            give(which, ref, src, slot(1, dy), x_bwd)

    def pass_on(which, ref, where, axis):
        dx, dy = where
        src = ref.at[slot(dx, dy)]
        if axis == "x":
            if dx == 3:
                give(which, ref, src, slot(2, dy), x_fwd, 0)
            else:
                give(which, ref, src, slot(2, dy), x_bwd, 1)
        else:
            if dy == 3:
                give(which, ref, src, slot(dx, 2), y_fwd, 0)
            else:
                give(which, ref, src, slot(dx, 2), y_bwd, 1)

    def both_halves(which, where):
        got(which, where, 0)
        got(which, where, 1)

    def pack_pair(p):
        s0, s1 = slot(*PAIRS[p][0]), slot(*PAIRS[p][1])
        for ref, dense in ((slot_in, dense_in), (slot_out, dense_out)):
            both = jnp.concatenate([ref[s0].astype(F32), ref[s1].astype(F32)], axis=0)
            dense[p] = both.astype(BF16)

    def forward_pair(p):
        pack_pair(p)

        @pl.loop(0, 2)
        def _(i):
            rows = pl.ds(2 * i, 2)
            pre = mm_nt(x[rows].reshape(4 * R, D), dense_in[p])
            act, der = gelu_and_slope(pre)
            slope[p, rows] = der.astype(slope.dtype).reshape(2, 2 * R, 2 * U)
            act = act.astype(BF16)
            for n in range(0, D, 256):
                part = mm(act, dense_out[p, :, n:n + 256]).reshape(2, 2 * R, 256)
                if p == 0:
                    acc[rows, :, n:n + 256] = part
                else:
                    acc[rows, :, n:n + 256] += part

    for dx in (3, 1):
        got("in", (dx, 0))
        pass_on(*A, (dx, 0), "x")
    for dy in (3, 1):
        got("out", (0, dy))
        pass_on(*B, (0, dy), "y")
    for dx in (3, 1):
        spread(*A, (dx, 0), "y")
    for dy in (3, 1):
        spread(*B, (0, dy), "x")
    for copy in locals_:
        copy.wait()
    for dy in (3, 1):
        got("in", (0, dy))
        pass_on(*A, (0, dy), "y")
    for dx in (3, 1):
        got("out", (dx, 0))
        pass_on(*B, (dx, 0), "x")
    x_up.wait_recv()
    x_down.wait_recv()
    for copy in text_first:
        copy.wait_recv()
    text_far = send(tall.at[0], tall.at[1], z_far)
    text_core = send(tall.at[0], tall.at[2], core)
    forward_pair(0)
    both_halves("in", (2, 0))
    spread(*A, (2, 0), "y")
    both_halves("out", (0, 2))
    spread(*B, (0, 2), "x")
    forward_pair(1)
    for dx in (3, 1):
        for dy in (3, 1):
            got("in", (dx, dy))
            pass_on(*A, (dx, dy), "y")
    for dy in (3, 1):
        for dx in (3, 1):
            got("out", (dx, dy))
            pass_on(*B, (dx, dy), "x")
    forward_pair(2)
    text_far.wait_recv()
    text_far_core = send(tall.at[1], tall.at[3], core)
    forward_pair(3)
    both_halves("in", (0, 2))
    both_halves("out", (2, 0))
    for dy in (3, 1):
        got("in", (2, dy))
        pass_on(*A, (2, dy), "y")
    for dx in (3, 1):
        got("out", (dx, 2))
        pass_on(*B, (dx, 2), "x")
    forward_pair(4)
    both_halves("out", (2, 3))
    forward_pair(5)
    both_halves("out", (2, 1))
    both_halves("in", (3, 2))
    forward_pair(6)
    both_halves("in", (1, 2))
    both_halves("in", (2, 2))
    both_halves("out", (2, 2))
    forward_pair(7)

    lo, hi = slice(0, H), slice(H, D)

    def reduce_rows(turn):
        from_core = {}
        for dz in (2, 1, 3, 0):
            stage[turn, dz] = acc[dz, R:2 * R, :].astype(BF16)
            from_core[dz] = send(stage.at[turn, dz], core_in.at[turn, dz], core)
        from_core[2].wait_recv()
        direct[turn, 0] = (acc[2, :R, :] + core_in[turn, 2].astype(F32)).astype(BF16)
        hop_up = send(direct.at[turn, 0, :, lo], hop.at[turn, 0], z_fwd)
        hop_down = send(direct.at[turn, 0, :, hi], hop.at[turn, 1], z_bwd)
        from_core[1].wait_recv()
        up = acc[1, :R, :] + core_in[turn, 1].astype(F32)
        acc[1, :R, :] = up
        direct[turn, 1, :, hi] = up[:, hi].astype(BF16)
        up_hi = send(direct.at[turn, 1, :, hi], fin.at[turn, 0, :, hi], z_fwd)
        from_core[3].wait_recv()
        down = acc[3, :R, :] + core_in[turn, 3].astype(F32)
        acc[3, :R, :] = down
        direct[turn, 2, :, lo] = down[:, lo].astype(BF16)
        down_lo = send(direct.at[turn, 2, :, lo], fin.at[turn, 1, :, lo], z_bwd)
        from_core[0].wait_recv()
        acc[0, :R, :] += core_in[turn, 0].astype(F32)
        hop_up.wait_recv()
        direct[turn, 1, :, lo] = (acc[1, :R, lo] + hop[turn, 0].astype(F32)).astype(BF16)
        up_lo = send(direct.at[turn, 1, :, lo], fin.at[turn, 0, :, lo], z_fwd)
        hop_down.wait_recv()
        direct[turn, 2, :, hi] = (acc[3, :R, hi] + hop[turn, 1].astype(F32)).astype(BF16)
        down_hi = send(direct.at[turn, 2, :, hi], fin.at[turn, 1, :, hi], z_bwd)
        return up_hi, down_lo, up_lo, down_hi

    def reduced(turn, pending):
        for copy in pending:
            copy.wait_recv()
        return acc[0, :R, :] + fin[turn, 0].astype(F32) + fin[turn, 1].astype(F32)

    pending = reduce_rows(0)
    mixed = reduced(0, pending)
    pooled_rows = pooled[pl.ds(pl.multiple_of(own_row, 16), R), :].astype(F32)
    resid_bf[...] = (pooled_rows + mixed).astype(BF16)

    own_cols = pl.ds(pl.multiple_of(z_lo * H, 128), H)
    other_cols = pl.ds(pl.multiple_of((1 - z_lo) * H, 128), H)
    rs[0, 0] = resid_bf[:, own_cols]
    rs_up = send(resid_bf.at[:, other_cols], rs.at[0, 3], z_fwd)
    rs_down = send(resid_bf.at[:, other_cols], rs.at[0, 1], z_bwd)
    rs_hop_up = send(resid_bf.at[0:48, own_cols], rs_hop.at[0:48], z_fwd)
    rs_hop_down = send(resid_bf.at[48:80, own_cols], rs_hop.at[48:80], z_bwd)

    project = mm(resid_bf[...], proj[...])
    inverse = lax.rsqrt(jnp.sum(project * project, axis=-1, keepdims=True) + 1e-06)
    unit_f = project * inverse
    embeds = unit_f.astype(BF16)
    eall[0, 0] = embeds
    embeds_first = [send(eall.at[0, 0], eall.at[0, k], shifted(-k)) for k in (1, 2, 3)]

    text_core.wait_recv()
    text_far_core.wait_recv()
    scaling = scale[0]
    offset = bias[0]
    same = lax.broadcasted_iota(jnp.int32, (R, R), 0) == lax.broadcasted_iota(jnp.int32, (R, R), 1)

    def coefs(mine, theirs, q):
        out = []
        for k in range(4):
            logits = scaling * mm_nt(mine, theirs[q, k]) + offset
            soft = jax.nn.sigmoid(logits)
            if q == 0 and k == 0:
                soft = jnp.where(same, -jax.nn.sigmoid(-logits), soft)
            out.append(soft.astype(BF16))
        return out

    def other_side(mine, theirs):
        total = None
        for q in range(4):
            for k, coef in enumerate(coefs(mine, theirs, q)):
                term = mm(coef, theirs[q, k])
                total = term if total is None else total + term
        return scaling * total

    embed_grad = other_side(embeds, tall)
    inner = jnp.sum(unit_f * embed_grad, axis=-1, keepdims=True)
    pd[0, 0] = (inverse * (embed_grad - unit_f * inner)).astype(BF16)
    pd_up = send(pd.at[0, 0], pd.at[0, 3], z_fwd)
    pd_down = send(pd.at[0, 0], pd.at[0, 1], z_bwd)
    pd_core = {0: send(pd.at[0, 0], pd.at[1, 0], core)}
    resid_grad[...] = mm_nt(pd[0, 0], proj[...])
    grad_bf[0, :R, :] = resid_grad[...].astype(BF16)
    pd_core[0].wait_recv()
    grad_bf[0, R:, :] = mm_nt(pd[1, 0], proj[...]).astype(BF16)

    pd_up.wait_recv()
    pd_far_up = send(pd.at[0, 3, :, 0:512], pd.at[0, 2, :, 0:512], z_fwd)
    pd_core[3] = send(pd.at[0, 3], pd.at[1, 3], core)
    pd_down.wait_recv()
    pd_far_down = send(pd.at[0, 1, :, 512:1024], pd.at[0, 2, :, 512:1024], z_bwd)
    pd_core[1] = send(pd.at[0, 1], pd.at[1, 1], core)

    def expand(dz):
        both = jnp.concatenate([pd[0, dz], pd[1, dz]], axis=0)
        grad_bf[dz] = mm_nt(both, proj[...]).astype(BF16)

    for dz in (3, 1):
        pd_core[dz].wait_recv()
        expand(dz)
    pd_far_up.wait_recv()
    pd_far_down.wait_recv()
    pd_core[2] = send(pd.at[0, 2], pd.at[1, 2], core)
    for copy in embeds_first:
        copy.wait_recv()
    embeds_far = send(eall.at[0], eall.at[1], z_far)
    embeds_core = send(eall.at[0], eall.at[2], core)
    rs_hop_up.wait_recv()
    rs_far_up = send(rs_hop.at[0:48], rs.at[0, 2, 0:48], z_fwd)
    rs_hop_down.wait_recv()
    rs_far_down = send(rs_hop.at[48:80], rs.at[0, 2, 48:80], z_bwd)
    pd_core[2].wait_recv()
    expand(2)

    @pl.loop(0, 8)
    def _(p):
        @pl.loop(0, 2)
        def _(i):
            rows = pl.ds(2 * i, 2)
            act_grad = mm_nt(grad_bf[rows].reshape(4 * R, D), dense_out[p])
            pre_grad = (act_grad * slope[p, rows].reshape(4 * R, 2 * U).astype(F32)).astype(BF16)
            for n in range(0, D, 256):
                part = mm(pre_grad, dense_in[p, :, n:n + 256]).reshape(2, 2 * R, 256)

                @pl.when(p == 0)
                def _():
                    acc[rows, :, n:n + 256] = part

                @pl.when(p > 0)
                def _():
                    acc[rows, :, n:n + 256] += part

    rs_up.wait_recv()
    rs_down.wait_recv()
    rs_far_up.wait_recv()
    rs_far_down.wait_recv()
    rs_core = send(rs.at[0], rs.at[1], core)
    embeds_far.wait_recv()
    embeds_far_core = send(eall.at[1], eall.at[3], core)
    pending = reduce_rows(1)
    rs_core.wait_recv()
    columns = pl.ds(pl.multiple_of(mp * 256, 128), 256)
    term = mm_tn(rs[...].reshape(8 * R, H), pd[:, :, :, columns].reshape(8 * R, 256))
    for n in range(16):
        pg[n % 4, n // 4] = term[n * 56:(n + 1) * 56, :].astype(BF16)
    pg_first = [
        send(pg.at[(xi + k) % 4], pg_in.at[k - 1], where)
        for k, where in ((1, x_fwd), (2, x_far), (3, x_bwd))
    ]

    embeds_core.wait_recv()
    embeds_far_core.wait_recv()
    tf, text_inv = text_parts()
    unit_grad = other_side(tall[0, 0], eall)
    text_grad[...] = text_inv * (
        unit_grad - tf * jnp.sum(tf * unit_grad, axis=-1, keepdims=True)
    )

    for copy in pg_first:
        copy.wait_recv()
    part = pg[xi].astype(F32)
    for k in range(3):
        part = part + pg_in[k].astype(F32)
    pg2[...] = part.astype(BF16)
    pg_second = [
        send(pg2.at[(yi + k) % 4], pg2_in.at[k - 1], where)
        for k, where in ((1, y_fwd), (2, y_far), (3, y_bwd))
    ]

    input_grad = reduced(1, pending)
    _, normed, inv_std = norm_rows(own_row)
    scaled = input_grad * gain[...]
    shift = scaled - jnp.mean(scaled, axis=-1, keepdims=True)
    shift = shift - normed * jnp.mean(scaled * normed, axis=-1, keepdims=True)
    d_pooled[...] = resid_grad[...] + inv_std * shift

    for copy in pg_second:
        copy.wait_recv()
    out = pg2[yi].astype(F32)
    for k in range(3):
        out = out + pg2_in[k].astype(F32)
    proj_grad[...] = out

    for copy in started:
        copy.wait_send()


def per_device(pooled, ln_gain, w_in, w_out, proj, text, logit_scale, logit_bias):
    vmem = pl.BlockSpec(memory_space=pltpu.VMEM)
    smem = pl.BlockSpec(memory_space=pltpu.SMEM)
    hbm = pl.BlockSpec(memory_space=pl.ANY)
    return pl.pallas_call(
        kernel,
        out_shape=(
            jax.ShapeDtypeStruct((R, D), F32),
            jax.ShapeDtypeStruct((56, 256), F32),
            jax.ShapeDtypeStruct((R, E), F32),
        ),
        in_specs=[vmem, vmem, hbm, hbm, hbm, vmem, smem, smem],
        out_specs=(vmem, vmem, vmem),
        scratch_shapes=[
            pltpu.VMEM((16, U, D), BF16),
            pltpu.VMEM((16, U, D), BF16),
            pltpu.VMEM((8, 2 * U, D), BF16),
            pltpu.VMEM((8, 2 * U, D), BF16),
            pltpu.VMEM((4, 2 * R, D), BF16),
            pltpu.VMEM((4, 2 * R, D), F32),
            pltpu.VMEM((8, 4, 2 * R, 2 * U), BF16),
            pltpu.VMEM((4, 2 * R, D), BF16),
            pltpu.VMEM((R, D), F32),
            pltpu.VMEM((4, 4, R, E), BF16),
            pltpu.VMEM((4, 4, R, E), BF16),
            pltpu.VMEM((D, E), BF16),
            pltpu.VMEM((2, 4, R, D), BF16),
            pltpu.VMEM((2, 4, R, D), BF16),
            pltpu.VMEM((2, 2, R, H), BF16),
            pltpu.VMEM((2, 2, R, D), BF16),
            pltpu.VMEM((2, 3, R, D), BF16),
            pltpu.VMEM((2, 4, R, E), BF16),
            pltpu.VMEM((R, D), BF16),
            pltpu.VMEM((2, 4, R, H), BF16),
            pltpu.VMEM((R, H), BF16),
            pltpu.VMEM((4, 4, 56, 256), BF16),
            pltpu.VMEM((3, 4, 56, 256), BF16),
            pltpu.VMEM((4, 56, 256), BF16),
            pltpu.VMEM((3, 56, 256), BF16),
            pltpu.SemaphoreType.DMA((N_SEMS,)),
            pltpu.SemaphoreType.DMA((N_SEMS,)),
            pltpu.SemaphoreType.DMA((3,)),
        ],
        compiler_params=pltpu.CompilerParams(
            collective_id=0, has_side_effects=True, vmem_limit_bytes=66 * 1000 * 1000
        ),
    )(pooled, ln_gain.reshape(1, D), w_in, w_out, proj, text, logit_scale, logit_bias)


def solution(mesh):
    in_specs = (
        P("dp", None),
        P(),
        P(("dp", "mp"), None),
        P(("dp", "mp"), None),
        P(),
        P(("dp", "mp"), None),
        P(),
        P(),
    )
    out_specs = (P(("dp", "mp"), None), P("dp", "mp"), P(("dp", "mp"), None))
    return jax.shard_map(
        per_device, mesh=mesh, in_specs=in_specs, out_specs=out_specs, check_vma=False
    )
```

```python
import functools

import jax
import jax.numpy as jnp
from jax import lax
from jax.experimental import pallas as pl
from jax.experimental.pallas import tpu as pltpu
from jax.sharding import PartitionSpec as P

D = 1792
H = D // 2
E = 1024
U = 120
R = 80
F32 = jnp.float32
BF16 = jnp.bfloat16
MESH = pl.DeviceIdType.MESH
PAIRS = (
    ((0, 0), (3, 0)),
    ((1, 0), (0, 3)),
    ((0, 1), (3, 3)),
    ((3, 1), (1, 3)),
    ((1, 1), (2, 0)),
    ((0, 2), (2, 3)),
    ((2, 1), (3, 2)),
    ((1, 2), (2, 2)),
)
PLACE = {0: 0, 1: 1, 3: 2, 2: 3}
N_SEMS = 128


def mm(a, b):
    return lax.dot_general(a, b, (((1,), (0,)), ((), ())), preferred_element_type=F32)


def mm_nt(a, b):
    return lax.dot_general(a, b, (((1,), (1,)), ((), ())), preferred_element_type=F32)


def mm_tn(a, b):
    return lax.dot_general(a, b, (((0,), (0,)), ((), ())), preferred_element_type=F32)


def gelu_and_slope(v):
    c = 0.7978845608028654
    v2 = v * v
    t = jnp.tanh(c * v * (1.0 + 0.044715 * v2))
    half = 0.5 * (1.0 + t)
    act = v * half
    slope = half + (0.5 * v) * (1.0 - t * t) * (c * (1.0 + 3.0 * 0.044715 * v2))
    return act, slope


def kernel(
    pooled, gain, w_in, w_out, proj_hbm, text, scale, bias,
    d_pooled, proj_grad, text_grad,
    slot_in, slot_out, dense_in, dense_out, x, acc, slope, resid_grad,
    tall, eall, proj, stage, core_in, hop, fin, direct, pd, resid_bf, rs, unit_part,
    pg, pg_in, pg2, pg2_in, send_sems, recv_sems, local_sems,
):
    dp = lax.axis_index("dp")
    mp = lax.axis_index("mp")
    z_lo = dp // 16
    yi = (dp // 4) % 4
    xi = dp % 4
    z_hi = mp // 2
    c = mp % 2
    z = z_hi * 2 + z_lo

    def place(dx=0, dy=0, dz=0, other=False):
        nz = (z + dz) % 4
        ndp = (nz % 2) * 16 + ((yi + dy) % 4) * 4 + (xi + dx) % 4
        nmp = (nz // 2) * 2 + (1 - c if other else c)
        return {"dp": ndp, "mp": nmp}

    def shifted(k):
        return {"dp": (dp + k + 32) % 32, "mp": mp}

    along_x = {k: place(dx=k) for k in (3, 1, 2)}
    along_y = {k: place(dy=k) for k in (3, 1, 2)}
    z_fwd, z_bwd, z_far = place(dz=1), place(dz=3), place(dz=2)
    core = place(other=True)

    count = [0]
    started = []

    def send(src, dst, where):
        n = count[0]
        count[0] += 1
        copy = pltpu.make_async_remote_copy(
            src_ref=src, dst_ref=dst, send_sem=send_sems.at[n], recv_sem=recv_sems.at[n],
            device_id=where, device_id_type=MESH,
        )
        copy.start()
        started.append(copy)
        return copy

    def sent(copies):
        for copy in copies:
            copy.wait_send()
            started[:] = [other for other in started if other is not copy]

    def arrived(copies):
        for copy in copies:
            copy.wait_recv()

    def slot(dx, dy):
        return dy * 4 + dx

    locals_ = [
        pltpu.make_async_copy(w_in, slot_in.at[0], local_sems.at[0]),
        pltpu.make_async_copy(w_out, slot_out.at[0], local_sems.at[1]),
        pltpu.make_async_copy(proj_hbm, proj, local_sems.at[2]),
    ]
    for copy in locals_:
        copy.start()

    peers = list(along_x.values()) + list(along_y.values()) + [z_fwd, z_bwd, z_far, core]
    peers += [shifted(k) for k in (-3, -2, -1, 1, 2, 3)]
    barrier = pltpu.get_barrier_semaphore()
    for peer in peers:
        pl.semaphore_signal(barrier, inc=1, device_id=peer, device_id_type=MESH)
    pl.semaphore_wait(barrier, len(peers))

    arrive = {}

    def give(which, src, at, where, half=None):
        target = (slot_in if which == "in" else slot_out).at[slot(*at)]
        if half is not None:
            columns = pl.ds(half * H, H)
            target, src = target.at[:, columns], src.at[:, columns]
        arrive[which, at, half] = send(src, target, where)

    def held(which, at):
        return (slot_in if which == "in" else slot_out).at[slot(*at)]

    def got(which, at, half=None):
        arrive[which, at, half].wait_recv()

    def got_halves(which, at):
        got(which, at, 0)
        got(which, at, 1)

    def give_both_ways(which, at, axis, src=None):
        src = held(which, at) if src is None else src
        if axis == "x":
            give(which, src, ((at[0] + 3) % 4, at[1]), along_x[1])
            give(which, src, ((at[0] + 1) % 4, at[1]), along_x[3])
        else:
            give(which, src, (at[0], (at[1] + 3) % 4), along_y[1])
            give(which, src, (at[0], (at[1] + 1) % 4), along_y[3])

    def pass_on(which, at, axis):
        dx, dy = at
        src = held(which, at)
        if axis == "x":
            k, half = (1, 0) if dx == 3 else (3, 1)
            give(which, src, (2, dy), along_x[k], half)
        else:
            k, half = (1, 0) if dy == 3 else (3, 1)
            give(which, src, (dx, 2), along_y[k], half)

    give_both_ways("in", (0, 0), "x", w_in)
    give_both_ways("out", (0, 0), "y", w_out)
    give_both_ways("out", (0, 0), "x", w_out)
    give_both_ways("in", (0, 0), "y", w_in)

    def norm_rows(start):
        h = pooled[pl.ds(pl.multiple_of(start, 16), R), :].astype(F32)
        center = h - jnp.mean(h, axis=-1, keepdims=True)
        inv_std = lax.rsqrt(jnp.mean(center * center, axis=-1, keepdims=True) + 1e-06)
        return h, center * inv_std, inv_std

    own_row = z_hi * 160 + c * R
    other_row = z_hi * 160 + (1 - c) * R
    far_own = (1 - z_hi) * 160 + c * R
    far_other = (1 - z_hi) * 160 + (1 - c) * R

    def fill_x(dz, j, start):
        x[PLACE[dz], j * R:(j + 1) * R, :] = (norm_rows(start)[1] * gain[...]).astype(BF16)

    fill_x(0, 0, own_row)
    fill_x(0, 1, other_row)
    x_up = send(x.at[PLACE[0]], x.at[PLACE[3]], z_fwd)
    x_down = send(x.at[PLACE[0]], x.at[PLACE[1]], z_bwd)

    def text_parts():
        t = text[...].astype(F32)
        inv = lax.rsqrt(jnp.sum(t * t, axis=-1, keepdims=True) + 1e-06)
        return t * inv, inv

    tall[0, 0] = text_parts()[0].astype(BF16)
    text_far = send(tall.at[0, 0], tall.at[1, 0], z_far)
    fill_x(2, 0, far_own)
    fill_x(2, 1, far_other)

    def forward_pair(p):
        s0, s1 = slot(*PAIRS[p][0]), slot(*PAIRS[p][1])
        for ref, dense in ((slot_in, dense_in), (slot_out, dense_out)):
            both = jnp.concatenate([ref[s0].astype(F32), ref[s1].astype(F32)], axis=0)
            dense[p] = both.astype(BF16)
        pre = mm_nt(x[...].reshape(8 * R, D), dense_in[p])
        act, der = gelu_and_slope(pre)
        slope[p] = der.astype(BF16).reshape(4, 2 * R, 2 * U)
        act = act.astype(BF16)
        for n in range(0, D, 256):
            part = mm(act, dense_out[p, :, n:n + 256]).reshape(4, 2 * R, 256)
            if p == 0:
                acc[:, :, n:n + 256] = part
            else:
                acc[:, :, n:n + 256] += part

    for copy in locals_:
        copy.wait()
    for k in (3, 1):
        got("in", (k, 0))
        pass_on("in", (k, 0), "x")
        got("out", (0, k))
        pass_on("out", (0, k), "y")
    for k in (3, 1):
        give_both_ways("in", (k, 0), "y")
        give_both_ways("out", (0, k), "x")
    for k in (3, 1):
        got("in", (0, k))
        pass_on("in", (0, k), "y")
        got("out", (k, 0))
        pass_on("out", (k, 0), "x")
    arrived([x_up, x_down])
    sent([x_up, x_down])
    text_far.wait_recv()
    text_core = [send(tall.at[0:2, 0], tall.at[2:4, 0], core)]
    forward_pair(0)
    got_halves("in", (2, 0))
    give_both_ways("in", (2, 0), "y")
    got_halves("out", (0, 2))
    give_both_ways("out", (0, 2), "x")
    forward_pair(1)
    for j in (3, 1):
        for k in (3, 1):
            got("in", (j, k))
            pass_on("in", (j, k), "y")
            got("out", (k, j))
            pass_on("out", (k, j), "x")
    forward_pair(2)
    forward_pair(3)
    got_halves("in", (0, 2))
    got_halves("out", (2, 0))
    for k in (3, 1):
        got("in", (2, k))
        pass_on("in", (2, k), "y")
        got("out", (k, 2))
        pass_on("out", (k, 2), "x")
    forward_pair(4)
    got_halves("out", (2, 3))
    forward_pair(5)
    got_halves("out", (2, 1))
    got_halves("in", (3, 2))
    forward_pair(6)
    got_halves("in", (1, 2))
    got_halves("in", (2, 2))
    got_halves("out", (2, 2))
    text_next = [send(tall.at[0:2, 0], tall.at[0:2, k], shifted(k)) for k in (1, 3, 2)]
    forward_pair(7)

    lo, hi = slice(0, H), slice(H, D)
    own, other = slice(0, R), slice(R, 2 * R)

    class Rows:
        def __init__(self, turn):
            self.turn = turn
            self.core = {}
            self.last = []

        def offer(self, dz):
            stage[dz] = acc[PLACE[dz], other, :].astype(BF16)
            self.core[dz] = send(stage.at[dz], core_in.at[self.turn, dz], core)

        def both(self, dz, columns):
            theirs = core_in[self.turn, dz, :, columns].astype(F32)
            return acc[PLACE[dz], own, columns] + theirs

        def far(self):
            turn = self.turn
            self.core[2].wait_recv()
            direct[0] = self.both(2, slice(0, D)).astype(BF16)
            self.up = send(direct.at[0, :, lo], hop.at[turn, 0], z_fwd)
            self.down = send(direct.at[0, :, hi], hop.at[turn, 1], z_bwd)

        def near_up(self):
            turn = self.turn
            self.core[1].wait_recv()
            direct[1, :, hi] = self.both(1, hi).astype(BF16)
            self.last.append(send(direct.at[1, :, hi], fin.at[turn, 0, :, hi], z_fwd))

        def near_down(self):
            turn = self.turn
            self.core[3].wait_recv()
            direct[2, :, lo] = self.both(3, lo).astype(BF16)
            self.last.append(send(direct.at[2, :, lo], fin.at[turn, 1, :, lo], z_bwd))

        def hops(self):
            turn = self.turn
            self.up.wait_recv()
            total = self.both(1, lo) + hop[turn, 0].astype(F32)
            direct[1, :, lo] = total.astype(BF16)
            self.last.append(send(direct.at[1, :, lo], fin.at[turn, 0, :, lo], z_fwd))
            self.down.wait_recv()
            total = self.both(3, hi) + hop[turn, 1].astype(F32)
            direct[2, :, hi] = total.astype(BF16)
            self.last.append(send(direct.at[2, :, hi], fin.at[turn, 1, :, hi], z_bwd))

        def result(self):
            turn = self.turn
            self.core[0].wait_recv()
            mine = self.both(0, slice(0, D))
            arrived(self.last)
            return mine + fin[turn, 0].astype(F32) + fin[turn, 1].astype(F32)

    rows = Rows(0)
    for dz in (2, 1, 3, 0):
        rows.offer(dz)
    rows.far()
    rows.near_up()
    rows.near_down()
    rows.hops()
    mixed = rows.result()
    pooled_rows = pooled[pl.ds(pl.multiple_of(own_row, 16), R), :].astype(F32)
    resid_bf[...] = (pooled_rows + mixed).astype(BF16)

    own_cols = pl.ds(pl.multiple_of(z_lo * H, 128), H)
    other_cols = pl.ds(pl.multiple_of((1 - z_lo) * H, 128), H)
    project = mm(resid_bf[...], proj[...])
    inverse = lax.rsqrt(jnp.sum(project * project, axis=-1, keepdims=True) + 1e-06)
    unit_f = project * inverse
    embeds = unit_f.astype(BF16)
    eall[0, 0] = embeds
    embeds_first = [send(eall.at[0, 0], eall.at[0, k], shifted(-k)) for k in (1, 2, 3)]

    for n, k in enumerate((1, 3, 2)):
        text_next[n].wait_recv()
        text_core.append(send(tall.at[0:2, k], tall.at[2:4, k], core))
    arrived(text_core)
    scaling = scale[0]
    offset = bias[0]
    same = lax.broadcasted_iota(jnp.int32, (R, R), 0) == lax.broadcasted_iota(jnp.int32, (R, R), 1)

    def other_side(mine, theirs, slabs, positive):
        total = None
        for n in range(4 * slabs):
            block = theirs[n // 4, n % 4]
            logits = scaling * mm_nt(mine, block) + offset
            soft = jax.nn.sigmoid(logits)
            if positive and n == 0:
                soft = jnp.where(same, -jax.nn.sigmoid(-logits), soft)
            term = mm(soft.astype(BF16), block)
            total = term if total is None else total + term
        return scaling * total

    grad_bf = x
    embed_grad = other_side(embeds, tall, 4, True)
    inner = jnp.sum(unit_f * embed_grad, axis=-1, keepdims=True)
    pd[0, 0] = (inverse * (embed_grad - unit_f * inner)).astype(BF16)
    pd_up = send(pd.at[0, 0], pd.at[0, PLACE[3]], z_fwd)
    pd_down = send(pd.at[0, 0], pd.at[0, PLACE[1]], z_bwd)
    pd_core = {0: send(pd.at[0, 0], pd.at[1, 0], core)}
    resid_grad[...] = mm_nt(pd[0, 0], proj[...])
    grad_bf[0, own, :] = resid_grad[...].astype(BF16)
    pd_core[0].wait_recv()
    grad_bf[0, other, :] = mm_nt(pd[1, 0], proj[...]).astype(BF16)

    def expand(first, last):
        both = pd[0:2, first:last]
        pieces = [both[j, n] for n in range(last - first) for j in range(2)]
        grads = mm_nt(jnp.concatenate(pieces, axis=0), proj[...])
        grad_bf[first:last] = grads.astype(BF16).reshape(last - first, 2 * R, D)

    def hidden_back(first, last):
        n = (last - first) * 2 * R
        for p in range(8):
            act_grad = mm_nt(grad_bf[first:last].reshape(n, D), dense_out[p])
            der = slope[p, first:last].reshape(n, 2 * U).astype(F32)
            slope[p, first:last] = (act_grad * der).astype(BF16).reshape(last - first, 2 * R, 2 * U)

    def input_back(dz):
        at = PLACE[dz]
        for n in range(0, D, 256):
            total = mm(slope[0, at], dense_in[0, :, n:n + 256])
            for p in range(1, 8):
                total = total + mm(slope[p, at], dense_in[p, :, n:n + 256])
            acc[at, :, n:n + 256] = total

    def pass_delta(dz):
        at = PLACE[dz]
        half, where = (pl.ds(0, E // 2), z_fwd) if dz == 3 else (pl.ds(E // 2, E // 2), z_bwd)
        on = send(pd.at[0, at, :, half], pd.at[0, PLACE[2], :, half], where)
        pd_core[dz] = send(pd.at[0, at], pd.at[1, at], core)
        return on

    hidden_back(0, 1)
    pd_up.wait_recv()
    pd_far = [pass_delta(3)]
    pd_down.wait_recv()
    pd_far.append(pass_delta(1))
    rs[0, 0] = resid_bf[:, own_cols]
    rs_in = [
        send(resid_bf.at[:, other_cols], rs.at[0, PLACE[3]], z_fwd),
        send(resid_bf.at[:, other_cols], rs.at[0, PLACE[1]], z_bwd),
        send(resid_bf.at[:, own_cols], rs.at[0, PLACE[2]], z_far),
    ]
    arrived(embeds_first)
    embeds_core = send(eall.at[0], eall.at[1], core)
    arrived([pd_core[3], pd_core[1]])
    expand(1, 3)
    arrived(pd_far)
    pd_core[2] = send(pd.at[0, PLACE[2]], pd.at[1, PLACE[2]], core)
    hidden_back(1, 3)
    embeds_core.wait_recv()
    unit_part[0] = other_side(tall[1, 0], eall, 2, False).astype(BF16)
    unit_far = send(unit_part.at[0], unit_part.at[1], z_far)
    pd_core[2].wait_recv()
    expand(3, 4)
    hidden_back(3, 4)

    sent(list(rows.core.values()) + rows.last + [rows.up, rows.down])
    rows = Rows(1)
    input_back(2)
    rows.offer(2)
    arrived(rs_in)
    rs_core = send(rs.at[0], rs.at[1], core)
    input_back(1)
    rows.offer(1)
    rows.far()
    input_back(3)
    rows.offer(3)
    rows.near_up()
    rows.near_down()

    rs_core.wait_recv()
    columns = pl.ds(pl.multiple_of(mp * 256, 128), 256)
    term = mm_tn(rs[...].reshape(8 * R, H), pd[:, :, :, columns].reshape(8 * R, 256))
    for n in range(16):
        pg[n % 4, n // 4] = term[n * 56:(n + 1) * 56, :].astype(BF16)
    pg_first = [send(pg.at[(xi + k) % 4], pg_in.at[k - 1], along_x[k]) for k in (1, 2, 3)]
    rows.hops()
    input_back(0)
    rows.offer(0)

    tf, text_inv = text_parts()
    unit_grad = other_side(tall[0, 0], eall, 2, True)
    unit_far.wait_recv()
    unit_grad = unit_grad + unit_part[1].astype(F32)
    text_grad[...] = text_inv * (
        unit_grad - tf * jnp.sum(tf * unit_grad, axis=-1, keepdims=True)
    )

    arrived(pg_first)
    part = pg[xi].astype(F32)
    for k in range(3):
        part = part + pg_in[k].astype(F32)
    pg2[...] = part.astype(BF16)
    pg_second = [send(pg2.at[(yi + k) % 4], pg2_in.at[k - 1], along_y[k]) for k in (1, 2, 3)]

    input_grad = rows.result()
    _, normed, inv_std = norm_rows(own_row)
    scaled = input_grad * gain[...]
    shift = scaled - jnp.mean(scaled, axis=-1, keepdims=True)
    shift = shift - normed * jnp.mean(scaled * normed, axis=-1, keepdims=True)
    d_pooled[...] = resid_grad[...] + inv_std * shift

    arrived(pg_second)
    out = pg2[yi].astype(F32)
    for k in range(3):
        out = out + pg2_in[k].astype(F32)
    proj_grad[...] = out

    for copy in started:
        copy.wait_send()


def per_device(pooled, ln_gain, w_in, w_out, proj, text, logit_scale, logit_bias):
    vmem = pl.BlockSpec(memory_space=pltpu.VMEM)
    smem = pl.BlockSpec(memory_space=pltpu.SMEM)
    hbm = pl.BlockSpec(memory_space=pl.ANY)
    return pl.pallas_call(
        kernel,
        out_shape=(
            jax.ShapeDtypeStruct((R, D), F32),
            jax.ShapeDtypeStruct((56, 256), F32),
            jax.ShapeDtypeStruct((R, E), F32),
        ),
        in_specs=[vmem, vmem, hbm, hbm, hbm, vmem, smem, smem],
        out_specs=(vmem, vmem, vmem),
        scratch_shapes=[
            pltpu.VMEM((16, U, D), BF16),
            pltpu.VMEM((16, U, D), BF16),
            pltpu.VMEM((8, 2 * U, D), BF16),
            pltpu.VMEM((8, 2 * U, D), BF16),
            pltpu.VMEM((4, 2 * R, D), BF16),
            pltpu.VMEM((4, 2 * R, D), F32),
            pltpu.VMEM((8, 4, 2 * R, 2 * U), BF16),
            pltpu.VMEM((R, D), F32),
            pltpu.VMEM((4, 4, R, E), BF16),
            pltpu.VMEM((2, 4, R, E), BF16),
            pltpu.VMEM((D, E), BF16),
            pltpu.VMEM((4, R, D), BF16),
            pltpu.VMEM((2, 4, R, D), BF16),
            pltpu.VMEM((2, 2, R, H), BF16),
            pltpu.VMEM((2, 2, R, D), BF16),
            pltpu.VMEM((3, R, D), BF16),
            pltpu.VMEM((2, 4, R, E), BF16),
            pltpu.VMEM((R, D), BF16),
            pltpu.VMEM((2, 4, R, H), BF16),
            pltpu.VMEM((2, R, E), BF16),
            pltpu.VMEM((4, 4, 56, 256), BF16),
            pltpu.VMEM((3, 4, 56, 256), BF16),
            pltpu.VMEM((4, 56, 256), BF16),
            pltpu.VMEM((3, 56, 256), BF16),
            pltpu.SemaphoreType.DMA((N_SEMS,)),
            pltpu.SemaphoreType.DMA((N_SEMS,)),
            pltpu.SemaphoreType.DMA((3,)),
        ],
        compiler_params=pltpu.CompilerParams(
            collective_id=0, has_side_effects=True, vmem_limit_bytes=64 * 1024 * 1024
        ),
    )(pooled, ln_gain.reshape(1, D), w_in, w_out, proj, text, logit_scale, logit_bias)


def solution(mesh):
    in_specs = (
        P("dp", None),
        P(),
        P(("dp", "mp"), None),
        P(("dp", "mp"), None),
        P(),
        P(("dp", "mp"), None),
        P(),
        P(),
    )
    out_specs = (P(("dp", "mp"), None), P("dp", "mp"), P(("dp", "mp"), None))
    return jax.shard_map(
        per_device, mesh=mesh, in_specs=in_specs, out_specs=out_specs, check_vma=False
    )
```

```python
import functools

import jax
import jax.numpy as jnp
from jax import lax
from jax.experimental import pallas as pl
from jax.experimental.pallas import tpu as pltpu
from jax.sharding import PartitionSpec as P

D = 1792
H = D // 2
E = 1024
U = 120
R = 80
F32 = jnp.float32
BF16 = jnp.bfloat16
MESH = pl.DeviceIdType.MESH
PAIRS = (
    ((0, 0), (3, 0)),
    ((1, 0), (0, 3)),
    ((0, 1), (3, 3)),
    ((3, 1), (1, 3)),
    ((1, 1), (2, 0)),
    ((0, 2), (2, 3)),
    ((2, 1), (3, 2)),
    ((1, 2), (2, 2)),
)
PLACE = {0: 0, 1: 1, 3: 2, 2: 3}
N_SEMS = 128


def mm(a, b):
    return lax.dot_general(a, b, (((1,), (0,)), ((), ())), preferred_element_type=F32)


def mm_nt(a, b):
    return lax.dot_general(a, b, (((1,), (1,)), ((), ())), preferred_element_type=F32)


def mm_tn(a, b):
    return lax.dot_general(a, b, (((0,), (0,)), ((), ())), preferred_element_type=F32)


def gelu_and_slope(v):
    c = 0.7978845608028654
    v2 = v * v
    t = jnp.tanh(c * v * (1.0 + 0.044715 * v2))
    half = 0.5 * (1.0 + t)
    act = v * half
    slope = half + (0.5 * v) * (1.0 - t * t) * (c * (1.0 + 3.0 * 0.044715 * v2))
    return act, slope


def kernel(
    pooled, gain, w_in, w_out, proj_hbm, text, scale, bias,
    d_pooled, proj_grad, text_grad,
    slot_in, slot_out, dense_in, dense_out, x, acc, slope, resid_grad,
    tall, eall, proj, stage, core_in, hop, fin, direct, pd, resid_bf, rs, unit_part,
    pg, pg_in, pg2, pg2_in, send_sems, recv_sems, local_sems,
):
    dp = lax.axis_index("dp")
    mp = lax.axis_index("mp")
    z_lo = dp // 16
    yi = (dp // 4) % 4
    xi = dp % 4
    z_hi = mp // 2
    c = mp % 2
    z = z_hi * 2 + z_lo

    def place(dx=0, dy=0, dz=0, other=False):
        nz = (z + dz) % 4
        ndp = (nz % 2) * 16 + ((yi + dy) % 4) * 4 + (xi + dx) % 4
        nmp = (nz // 2) * 2 + (1 - c if other else c)
        return {"dp": ndp, "mp": nmp}

    def shifted(k):
        return {"dp": (dp + k + 32) % 32, "mp": mp}

    along_x = {k: place(dx=k) for k in (3, 1, 2)}
    along_y = {k: place(dy=k) for k in (3, 1, 2)}
    z_fwd, z_bwd, z_far = place(dz=1), place(dz=3), place(dz=2)
    core = place(other=True)

    count = [0]
    started = []

    def send(src, dst, where):
        n = count[0]
        count[0] += 1
        copy = pltpu.make_async_remote_copy(
            src_ref=src, dst_ref=dst, send_sem=send_sems.at[n], recv_sem=recv_sems.at[n],
            device_id=where, device_id_type=MESH,
        )
        copy.start()
        started.append(copy)
        return copy

    def sent(copies):
        for copy in copies:
            copy.wait_send()
            started[:] = [other for other in started if other is not copy]

    def arrived(copies):
        for copy in copies:
            copy.wait_recv()

    def slot(dx, dy):
        return dy * 4 + dx

    locals_ = [
        pltpu.make_async_copy(w_in, slot_in.at[0], local_sems.at[0]),
        pltpu.make_async_copy(w_out, slot_out.at[0], local_sems.at[1]),
        pltpu.make_async_copy(proj_hbm, proj, local_sems.at[2]),
    ]
    for copy in locals_:
        copy.start()

    peers = list(along_x.values()) + list(along_y.values()) + [z_fwd, z_bwd, z_far, core]
    peers += [shifted(k) for k in (-3, -2, -1, 1, 2, 3)]
    barrier = pltpu.get_barrier_semaphore()
    for peer in peers:
        pl.semaphore_signal(barrier, inc=1, device_id=peer, device_id_type=MESH)
    pl.semaphore_wait(barrier, len(peers))

    arrive = {}

    def give(which, src, at, where, half=None):
        target = (slot_in if which == "in" else slot_out).at[slot(*at)]
        if half is not None:
            columns = pl.ds(half * H, H)
            target, src = target.at[:, columns], src.at[:, columns]
        arrive[which, at, half] = send(src, target, where)

    def held(which, at):
        return (slot_in if which == "in" else slot_out).at[slot(*at)]

    def got(which, at, half=None):
        arrive[which, at, half].wait_recv()

    def got_halves(which, at):
        got(which, at, 0)
        got(which, at, 1)

    def give_both_ways(which, at, axis, src=None):
        src = held(which, at) if src is None else src
        if axis == "x":
            give(which, src, ((at[0] + 3) % 4, at[1]), along_x[1])
            give(which, src, ((at[0] + 1) % 4, at[1]), along_x[3])
        else:
            give(which, src, (at[0], (at[1] + 3) % 4), along_y[1])
            give(which, src, (at[0], (at[1] + 1) % 4), along_y[3])

    def pass_on(which, at, axis):
        dx, dy = at
        src = held(which, at)
        if axis == "x":
            k, half = (1, 0) if dx == 3 else (3, 1)
            give(which, src, (2, dy), along_x[k], half)
        else:
            k, half = (1, 0) if dy == 3 else (3, 1)
            give(which, src, (dx, 2), along_y[k], half)

    give_both_ways("in", (0, 0), "x", w_in)
    give_both_ways("out", (0, 0), "y", w_out)
    give_both_ways("out", (0, 0), "x", w_out)
    give_both_ways("in", (0, 0), "y", w_in)

    def norm_rows(start):
        h = pooled[pl.ds(pl.multiple_of(start, 16), R), :].astype(F32)
        center = h - jnp.mean(h, axis=-1, keepdims=True)
        inv_std = lax.rsqrt(jnp.mean(center * center, axis=-1, keepdims=True) + 1e-06)
        return h, center * inv_std, inv_std

    own_row = z_hi * 160 + c * R
    other_row = z_hi * 160 + (1 - c) * R
    far_own = (1 - z_hi) * 160 + c * R
    far_other = (1 - z_hi) * 160 + (1 - c) * R

    def fill_x(dz, j, start):
        x[PLACE[dz], j * R:(j + 1) * R, :] = (norm_rows(start)[1] * gain[...].reshape(1, D)).astype(BF16)

    fill_x(0, 0, own_row)
    fill_x(0, 1, other_row)
    x_up = send(x.at[PLACE[0]], x.at[PLACE[3]], z_fwd)
    x_down = send(x.at[PLACE[0]], x.at[PLACE[1]], z_bwd)

    def text_parts():
        t = text[...].astype(F32)
        inv = lax.rsqrt(jnp.sum(t * t, axis=-1, keepdims=True) + 1e-06)
        return t * inv, inv

    tall[0, 0] = text_parts()[0].astype(BF16)
    text_first = [send(tall.at[0, 0], tall.at[0, k], shifted(k)) for k in (1, 2, 3)]
    fill_x(2, 0, far_own)
    fill_x(2, 1, far_other)

    def forward_pair(p):
        s0, s1 = slot(*PAIRS[p][0]), slot(*PAIRS[p][1])
        for ref, dense in ((slot_in, dense_in), (slot_out, dense_out)):
            both = jnp.concatenate([ref[s0].astype(F32), ref[s1].astype(F32)], axis=0)
            dense[p] = both.astype(BF16)
        pre = mm_nt(x[...].reshape(8 * R, D), dense_in[p])
        act, der = gelu_and_slope(pre)
        slope[p] = der.astype(BF16).reshape(4, 2 * R, 2 * U)
        act = act.astype(BF16)
        for n in range(0, D, 256):
            part = mm(act, dense_out[p, :, n:n + 256]).reshape(4, 2 * R, 256)
            if p == 0:
                acc[:, :, n:n + 256] = part
            else:
                acc[:, :, n:n + 256] += part

    for copy in locals_:
        copy.wait()
    for k in (3, 1):
        got("in", (k, 0))
        pass_on("in", (k, 0), "x")
        got("out", (0, k))
        pass_on("out", (0, k), "y")
    for k in (3, 1):
        give_both_ways("in", (k, 0), "y")
        give_both_ways("out", (0, k), "x")
    for k in (3, 1):
        got("in", (0, k))
        pass_on("in", (0, k), "y")
        got("out", (k, 0))
        pass_on("out", (k, 0), "x")
    arrived([x_up, x_down])
    sent([x_up, x_down])
    arrived(text_first)
    text_far = send(tall.at[0], tall.at[1], z_far)
    text_core = [send(tall.at[0], tall.at[2], core)]
    forward_pair(0)
    got_halves("in", (2, 0))
    give_both_ways("in", (2, 0), "y")
    got_halves("out", (0, 2))
    give_both_ways("out", (0, 2), "x")
    forward_pair(1)
    for j in (3, 1):
        for k in (3, 1):
            got("in", (j, k))
            pass_on("in", (j, k), "y")
            got("out", (k, j))
            pass_on("out", (k, j), "x")
    forward_pair(2)
    text_far.wait_recv()
    text_core.append(send(tall.at[1], tall.at[3], core))
    forward_pair(3)
    got_halves("in", (0, 2))
    got_halves("out", (2, 0))
    for k in (3, 1):
        got("in", (2, k))
        pass_on("in", (2, k), "y")
        got("out", (k, 2))
        pass_on("out", (k, 2), "x")
    forward_pair(4)
    got_halves("out", (2, 3))
    forward_pair(5)
    got_halves("out", (2, 1))
    got_halves("in", (3, 2))
    forward_pair(6)
    got_halves("in", (1, 2))
    got_halves("in", (2, 2))
    got_halves("out", (2, 2))
    forward_pair(7)

    lo, hi = slice(0, H), slice(H, D)
    own, other = slice(0, R), slice(R, 2 * R)

    class Rows:
        def __init__(self, turn):
            self.turn = turn
            self.core = {}
            self.last = []

        def offer(self, dz):
            stage[dz] = acc[PLACE[dz], other, :].astype(BF16)
            self.core[dz] = send(stage.at[dz], core_in.at[self.turn, dz], core)

        def both(self, dz, columns):
            theirs = core_in[self.turn, dz, :, columns].astype(F32)
            return acc[PLACE[dz], own, columns] + theirs

        def far(self):
            turn = self.turn
            self.core[2].wait_recv()
            direct[0] = self.both(2, slice(0, D)).astype(BF16)
            self.up = send(direct.at[0, :, lo], hop.at[turn, 0], z_fwd)
            self.down = send(direct.at[0, :, hi], hop.at[turn, 1], z_bwd)

        def near_up(self):
            turn = self.turn
            self.core[1].wait_recv()
            direct[1, :, hi] = self.both(1, hi).astype(BF16)
            self.last.append(send(direct.at[1, :, hi], fin.at[turn, 0, :, hi], z_fwd))

        def near_down(self):
            turn = self.turn
            self.core[3].wait_recv()
            direct[2, :, lo] = self.both(3, lo).astype(BF16)
            self.last.append(send(direct.at[2, :, lo], fin.at[turn, 1, :, lo], z_bwd))

        def hops(self):
            turn = self.turn
            self.up.wait_recv()
            total = self.both(1, lo) + hop[turn, 0].astype(F32)
            direct[1, :, lo] = total.astype(BF16)
            self.last.append(send(direct.at[1, :, lo], fin.at[turn, 0, :, lo], z_fwd))
            self.down.wait_recv()
            total = self.both(3, hi) + hop[turn, 1].astype(F32)
            direct[2, :, hi] = total.astype(BF16)
            self.last.append(send(direct.at[2, :, hi], fin.at[turn, 1, :, hi], z_bwd))

        def result(self):
            turn = self.turn
            self.core[0].wait_recv()
            mine = self.both(0, slice(0, D))
            arrived(self.last)
            return mine + fin[turn, 0].astype(F32) + fin[turn, 1].astype(F32)

    rows = Rows(0)
    for dz in (2, 1, 3, 0):
        rows.offer(dz)
    rows.far()
    rows.near_up()
    rows.near_down()
    rows.hops()
    mixed = rows.result()
    pooled_rows = pooled[pl.ds(pl.multiple_of(own_row, 16), R), :].astype(F32)
    resid_bf[...] = (pooled_rows + mixed).astype(BF16)

    own_cols = pl.ds(pl.multiple_of(z_lo * H, 128), H)
    other_cols = pl.ds(pl.multiple_of((1 - z_lo) * H, 128), H)
    rs[0, 0] = resid_bf[:, own_cols]
    rs_in = [
        send(resid_bf.at[:, other_cols], rs.at[0, PLACE[3]], z_fwd),
        send(resid_bf.at[:, other_cols], rs.at[0, PLACE[1]], z_bwd),
        send(resid_bf.at[:, own_cols], rs.at[0, PLACE[2]], z_far),
    ]

    project = mm(resid_bf[...], proj[...])
    inverse = lax.rsqrt(jnp.sum(project * project, axis=-1, keepdims=True) + 1e-06)
    unit_f = project * inverse
    embeds = unit_f.astype(BF16)
    eall[0, 0] = embeds

    arrived(text_core)
    scaling = scale[0]
    offset = bias[0]
    same = lax.broadcasted_iota(jnp.int32, (R, R), 0) == lax.broadcasted_iota(jnp.int32, (R, R), 1)

    def other_side(mine, theirs, slabs, positive):
        total = None
        for n in range(4 * slabs):
            block = theirs[n // 4, n % 4]
            logits = scaling * mm_nt(mine, block) + offset
            soft = jax.nn.sigmoid(logits)
            if positive and n == 0:
                soft = jnp.where(same, -jax.nn.sigmoid(-logits), soft)
            term = mm(soft.astype(BF16), block)
            total = term if total is None else total + term
        return scaling * total

    grad_bf = x
    embed_grad = other_side(embeds, tall, 4, True)
    inner = jnp.sum(unit_f * embed_grad, axis=-1, keepdims=True)
    pd[0, 0] = (inverse * (embed_grad - unit_f * inner)).astype(BF16)
    pd_up = send(pd.at[0, 0], pd.at[0, PLACE[3]], z_fwd)
    pd_down = send(pd.at[0, 0], pd.at[0, PLACE[1]], z_bwd)
    pd_core = {0: send(pd.at[0, 0], pd.at[1, 0], core)}
    resid_grad[...] = mm_nt(pd[0, 0], proj[...])
    grad_bf[0, own, :] = resid_grad[...].astype(BF16)
    pd_core[0].wait_recv()
    grad_bf[0, other, :] = mm_nt(pd[1, 0], proj[...]).astype(BF16)

    def expand(first, last):
        both = pd[0:2, first:last]
        pieces = [both[j, n] for n in range(last - first) for j in range(2)]
        grads = mm_nt(jnp.concatenate(pieces, axis=0), proj[...])
        grad_bf[first:last] = grads.astype(BF16).reshape(last - first, 2 * R, D)

    def hidden_back(first, last):
        n = (last - first) * 2 * R
        for p in range(8):
            act_grad = mm_nt(grad_bf[first:last].reshape(n, D), dense_out[p])
            der = slope[p, first:last].reshape(n, 2 * U).astype(F32)
            slope[p, first:last] = (act_grad * der).astype(BF16).reshape(last - first, 2 * R, 2 * U)

    def input_back(dz):
        at = PLACE[dz]
        for n in range(0, D, 256):
            total = mm(slope[0, at], dense_in[0, :, n:n + 256])
            for p in range(1, 8):
                total = total + mm(slope[p, at], dense_in[p, :, n:n + 256])
            acc[at, :, n:n + 256] = total

    def pass_delta(dz):
        at = PLACE[dz]
        half, where = (pl.ds(0, E // 2), z_fwd) if dz == 3 else (pl.ds(E // 2, E // 2), z_bwd)
        on = send(pd.at[0, at, :, half], pd.at[0, PLACE[2], :, half], where)
        pd_core[dz] = send(pd.at[0, at], pd.at[1, at], core)
        return on

    hidden_back(0, 1)
    pd_up.wait_recv()
    pd_far = [pass_delta(3)]
    pd_down.wait_recv()
    pd_far.append(pass_delta(1))
    embeds_first = [send(eall.at[0, 0], eall.at[0, k], shifted(-k)) for k in (1, 2, 3)]
    arrived([pd_core[3], pd_core[1]])
    expand(1, 3)
    arrived(pd_far)
    pd_core[2] = send(pd.at[0, PLACE[2]], pd.at[1, PLACE[2]], core)
    hidden_back(1, 3)
    pd_core[2].wait_recv()
    expand(3, 4)
    hidden_back(3, 4)

    sent(list(rows.core.values()) + rows.last + [rows.up, rows.down])
    rows = Rows(1)
    input_back(2)
    rows.offer(2)
    arrived(rs_in)
    rs_core = send(rs.at[0], rs.at[1], core)
    arrived(embeds_first)
    embeds_core = send(eall.at[0], eall.at[1], core)
    input_back(1)
    rows.offer(1)
    rows.far()
    input_back(3)
    rows.offer(3)
    rows.near_up()
    rows.near_down()

    rs_core.wait_recv()
    columns = pl.ds(pl.multiple_of(mp * 256, 128), 256)
    term = mm_tn(rs[...].reshape(8 * R, H), pd[:, :, :, columns].reshape(8 * R, 256))
    for n in range(16):
        pg[n % 4, n // 4] = term[n * 56:(n + 1) * 56, :].astype(BF16)
    pg_first = [send(pg.at[(xi + k) % 4], pg_in.at[k - 1], along_x[k]) for k in (1, 2, 3)]
    rows.hops()
    embeds_core.wait_recv()
    unit_part[0] = other_side(tall[1, 0], eall, 2, False).astype(BF16)
    unit_far = send(unit_part.at[0], unit_part.at[1], z_far)
    input_back(0)
    rows.offer(0)

    arrived(pg_first)
    part = pg[xi].astype(F32)
    for k in range(3):
        part = part + pg_in[k].astype(F32)
    pg2[...] = part.astype(BF16)
    pg_second = [send(pg2.at[(yi + k) % 4], pg2_in.at[k - 1], along_y[k]) for k in (1, 2, 3)]

    tf, text_inv = text_parts()
    unit_grad = other_side(tall[0, 0], eall, 2, True)
    input_grad = rows.result()
    _, normed, inv_std = norm_rows(own_row)
    scaled = input_grad * gain[...].reshape(1, D)
    shift = scaled - jnp.mean(scaled, axis=-1, keepdims=True)
    shift = shift - normed * jnp.mean(scaled * normed, axis=-1, keepdims=True)
    d_pooled[...] = resid_grad[...] + inv_std * shift

    unit_far.wait_recv()
    unit_grad = unit_grad + unit_part[1].astype(F32)
    text_grad[...] = text_inv * (
        unit_grad - tf * jnp.sum(tf * unit_grad, axis=-1, keepdims=True)
    )

    arrived(pg_second)
    out = pg2[yi].astype(F32)
    for k in range(3):
        out = out + pg2_in[k].astype(F32)
    proj_grad[...] = out

    for copy in started:
        copy.wait_send()


def write_out(d_in, p_in, t_in, d_out, p_out, t_out):
    d_out[...] = d_in[...]
    p_out[...] = p_in[...]
    t_out[...] = t_in[...]


def per_device(pooled, ln_gain, w_in, w_out, proj, text, logit_scale, logit_bias):
    vmem = pl.BlockSpec(memory_space=pltpu.VMEM)
    smem = pl.BlockSpec(memory_space=pltpu.SMEM)
    hbm = pl.BlockSpec(memory_space=pl.ANY)
    results = pl.pallas_call(
        kernel,
        out_shape=(
            jax.ShapeDtypeStruct((R, D), F32),
            jax.ShapeDtypeStruct((56, 256), F32),
            jax.ShapeDtypeStruct((R, E), F32),
        ),
        in_specs=[vmem, vmem, hbm, hbm, hbm, vmem, smem, smem],
        out_specs=(vmem, vmem, vmem),
        scratch_shapes=[
            pltpu.VMEM((16, U, D), BF16),
            pltpu.VMEM((16, U, D), BF16),
            pltpu.VMEM((8, 2 * U, D), BF16),
            pltpu.VMEM((8, 2 * U, D), BF16),
            pltpu.VMEM((4, 2 * R, D), BF16),
            pltpu.VMEM((4, 2 * R, D), F32),
            pltpu.VMEM((8, 4, 2 * R, 2 * U), BF16),
            pltpu.VMEM((R, D), F32),
            pltpu.VMEM((4, 4, R, E), BF16),
            pltpu.VMEM((2, 4, R, E), BF16),
            pltpu.VMEM((D, E), BF16),
            pltpu.VMEM((4, R, D), BF16),
            pltpu.VMEM((2, 4, R, D), BF16),
            pltpu.VMEM((2, 2, R, H), BF16),
            pltpu.VMEM((2, 2, R, D), BF16),
            pltpu.VMEM((3, R, D), BF16),
            pltpu.VMEM((2, 4, R, E), BF16),
            pltpu.VMEM((R, D), BF16),
            pltpu.VMEM((2, 4, R, H), BF16),
            pltpu.VMEM((2, R, E), BF16),
            pltpu.VMEM((4, 4, 56, 256), BF16),
            pltpu.VMEM((3, 4, 56, 256), BF16),
            pltpu.VMEM((4, 56, 256), BF16),
            pltpu.VMEM((3, 56, 256), BF16),
            pltpu.SemaphoreType.DMA((N_SEMS,)),
            pltpu.SemaphoreType.DMA((N_SEMS,)),
            pltpu.SemaphoreType.DMA((3,)),
        ],
        compiler_params=pltpu.CompilerParams(
            collective_id=0, has_side_effects=True, vmem_limit_bytes=64 * 1024 * 1024
        ),
    )(pooled, ln_gain, w_in, w_out, proj, text, logit_scale, logit_bias)
    return pl.pallas_call(
        write_out,
        out_shape=[jax.ShapeDtypeStruct(r.shape, r.dtype) for r in results],
        in_specs=[vmem] * 3,
        out_specs=[vmem] * 3,
    )(*results)


def solution(mesh):
    in_specs = (
        P("dp", None),
        P(),
        P(("dp", "mp"), None),
        P(("dp", "mp"), None),
        P(),
        P(("dp", "mp"), None),
        P(),
        P(),
    )
    out_specs = (P(("dp", "mp"), None), P("dp", "mp"), P(("dp", "mp"), None))
    return jax.shard_map(
        per_device, mesh=mesh, in_specs=in_specs, out_specs=out_specs, check_vma=False
    )
```

```python
import functools

import jax
import jax.numpy as jnp
from jax import lax
from jax.experimental import pallas as pl
from jax.experimental.pallas import tpu as pltpu
from jax.sharding import PartitionSpec as P

D = 1792
H = D // 2
E = 1024
U = 120
R = 80
F32 = jnp.float32
BF16 = jnp.bfloat16
MESH = pl.DeviceIdType.MESH
PAIRS = (
    ((0, 0), (3, 0)),
    ((1, 0), (0, 3)),
    ((0, 1), (3, 3)),
    ((3, 1), (1, 3)),
    ((1, 1), (2, 0)),
    ((0, 2), (2, 3)),
    ((2, 1), (3, 2)),
    ((1, 2), (2, 2)),
)
PLACE = {0: 0, 1: 1, 3: 2, 2: 3}
N_SEMS = 128


def mm(a, b):
    return lax.dot_general(a, b, (((1,), (0,)), ((), ())), preferred_element_type=F32)


def mm_nt(a, b):
    return lax.dot_general(a, b, (((1,), (1,)), ((), ())), preferred_element_type=F32)


def mm_tn(a, b):
    return lax.dot_general(a, b, (((0,), (0,)), ((), ())), preferred_element_type=F32)


def gelu_and_slope(v):
    c = 0.7978845608028654
    v2 = v * v
    t = jnp.tanh(c * v * (1.0 + 0.044715 * v2))
    half = 0.5 * (1.0 + t)
    act = v * half
    slope = half + (0.5 * v) * (1.0 - t * t) * (c * (1.0 + 3.0 * 0.044715 * v2))
    return act, slope


def kernel(
    pooled, gain, w_in, w_out, proj_hbm, text, scale, bias,
    d_pooled, proj_grad, text_grad,
    slot_in, slot_out, dense_in, dense_out, x, acc, slope, resid_grad,
    tall, eall, proj, stage, core_in, hop, fin, direct, pd, resid_bf, rs, unit_part,
    pg, pg_in, pg2, pg2_in, send_sems, recv_sems, local_sems,
):
    dp = lax.axis_index("dp")
    mp = lax.axis_index("mp")
    z_lo = dp // 16
    yi = (dp // 4) % 4
    xi = dp % 4
    z_hi = mp // 2
    c = mp % 2
    z = z_hi * 2 + z_lo

    def place(dx=0, dy=0, dz=0, other=False):
        nz = (z + dz) % 4
        ndp = (nz % 2) * 16 + ((yi + dy) % 4) * 4 + (xi + dx) % 4
        nmp = (nz // 2) * 2 + (1 - c if other else c)
        return {"dp": ndp, "mp": nmp}

    def shifted(k):
        return {"dp": (dp + k + 32) % 32, "mp": mp}

    along_x = {k: place(dx=k) for k in (3, 1, 2)}
    along_y = {k: place(dy=k) for k in (3, 1, 2)}
    z_fwd, z_bwd, z_far = place(dz=1), place(dz=3), place(dz=2)
    core = place(other=True)

    count = [0]
    started = []

    def send(src, dst, where):
        n = count[0]
        count[0] += 1
        copy = pltpu.make_async_remote_copy(
            src_ref=src, dst_ref=dst, send_sem=send_sems.at[n], recv_sem=recv_sems.at[n],
            device_id=where, device_id_type=MESH,
        )
        copy.start()
        started.append(copy)
        return copy

    def sent(copies):
        for copy in copies:
            copy.wait_send()
            started[:] = [other for other in started if other is not copy]

    def arrived(copies):
        for copy in copies:
            copy.wait_recv()

    def slot(dx, dy):
        return dy * 4 + dx

    locals_ = [
        pltpu.make_async_copy(w_in, slot_in.at[0], local_sems.at[0]),
        pltpu.make_async_copy(w_out, slot_out.at[0], local_sems.at[1]),
        pltpu.make_async_copy(proj_hbm, proj, local_sems.at[2]),
    ]
    for copy in locals_:
        copy.start()

    peers = list(along_x.values()) + list(along_y.values()) + [z_fwd, z_bwd, z_far, core]
    peers += [shifted(k) for k in (-3, -2, -1, 1, 2, 3)]
    barrier = pltpu.get_barrier_semaphore()
    for peer in peers:
        pl.semaphore_signal(barrier, inc=1, device_id=peer, device_id_type=MESH)
    pl.semaphore_wait(barrier, len(peers))

    arrive = {}

    def give(which, src, at, where, half=None):
        target = (slot_in if which == "in" else slot_out).at[slot(*at)]
        if half is not None:
            columns = pl.ds(half * H, H)
            target, src = target.at[:, columns], src.at[:, columns]
        arrive[which, at, half] = send(src, target, where)

    def held(which, at):
        return (slot_in if which == "in" else slot_out).at[slot(*at)]

    def got(which, at, half=None):
        arrive[which, at, half].wait_recv()

    def got_halves(which, at):
        got(which, at, 0)
        got(which, at, 1)

    def give_both_ways(which, at, axis, src=None):
        src = held(which, at) if src is None else src
        if axis == "x":
            give(which, src, ((at[0] + 3) % 4, at[1]), along_x[1])
            give(which, src, ((at[0] + 1) % 4, at[1]), along_x[3])
        else:
            give(which, src, (at[0], (at[1] + 3) % 4), along_y[1])
            give(which, src, (at[0], (at[1] + 1) % 4), along_y[3])

    def pass_on(which, at, axis):
        dx, dy = at
        src = held(which, at)
        if axis == "x":
            k, half = (1, 0) if dx == 3 else (3, 1)
            give(which, src, (2, dy), along_x[k], half)
        else:
            k, half = (1, 0) if dy == 3 else (3, 1)
            give(which, src, (dx, 2), along_y[k], half)

    give_both_ways("in", (0, 0), "x", w_in)
    give_both_ways("out", (0, 0), "y", w_out)
    give_both_ways("out", (0, 0), "x", w_out)
    give_both_ways("in", (0, 0), "y", w_in)

    def norm_rows(start):
        h = pooled[pl.ds(pl.multiple_of(start, 16), R), :].astype(F32)
        center = h - jnp.mean(h, axis=-1, keepdims=True)
        inv_std = lax.rsqrt(jnp.mean(center * center, axis=-1, keepdims=True) + 1e-06)
        return h, center * inv_std, inv_std

    own_row = z_hi * 160 + c * R
    other_row = z_hi * 160 + (1 - c) * R
    far_own = (1 - z_hi) * 160 + c * R
    far_other = (1 - z_hi) * 160 + (1 - c) * R

    def fill_x(dz, j, start):
        x[PLACE[dz], j * R:(j + 1) * R, :] = (norm_rows(start)[1] * gain[...].reshape(1, D)).astype(BF16)

    fill_x(0, 0, own_row)
    fill_x(0, 1, other_row)
    x_up = send(x.at[PLACE[0]], x.at[PLACE[3]], z_fwd)
    x_down = send(x.at[PLACE[0]], x.at[PLACE[1]], z_bwd)

    def text_parts():
        t = text[...].astype(F32)
        inv = lax.rsqrt(jnp.sum(t * t, axis=-1, keepdims=True) + 1e-06)
        return t * inv, inv

    tall[0, 0] = text_parts()[0].astype(BF16)
    text_first = [send(tall.at[0, 0], tall.at[0, k], shifted(k)) for k in (1, 2, 3)]
    fill_x(2, 0, far_own)
    fill_x(2, 1, far_other)

    lo, hi = slice(0, H), slice(H, D)
    own, other = slice(0, R), slice(R, 2 * R)

    class Rows:
        def __init__(self, turn):
            self.turn = turn
            self.core = {}
            self.last = []

        def offer(self, dz):
            stage[dz] = acc[PLACE[dz], other, :].astype(BF16)
            self.core[dz] = send(stage.at[dz], core_in.at[self.turn, dz], core)

        def both(self, dz, columns):
            theirs = core_in[self.turn, dz, :, columns].astype(F32)
            return acc[PLACE[dz], own, columns] + theirs

        def far(self):
            turn = self.turn
            self.core[2].wait_recv()
            direct[0] = self.both(2, slice(0, D)).astype(BF16)
            self.up = send(direct.at[0, :, lo], hop.at[turn, 0], z_fwd)
            self.down = send(direct.at[0, :, hi], hop.at[turn, 1], z_bwd)

        def near_up(self):
            turn = self.turn
            self.core[1].wait_recv()
            direct[1, :, hi] = self.both(1, hi).astype(BF16)
            self.last.append(send(direct.at[1, :, hi], fin.at[turn, 0, :, hi], z_fwd))

        def near_down(self):
            turn = self.turn
            self.core[3].wait_recv()
            direct[2, :, lo] = self.both(3, lo).astype(BF16)
            self.last.append(send(direct.at[2, :, lo], fin.at[turn, 1, :, lo], z_bwd))

        def hops(self):
            turn = self.turn
            self.up.wait_recv()
            total = self.both(1, lo) + hop[turn, 0].astype(F32)
            direct[1, :, lo] = total.astype(BF16)
            self.last.append(send(direct.at[1, :, lo], fin.at[turn, 0, :, lo], z_fwd))
            self.down.wait_recv()
            total = self.both(3, hi) + hop[turn, 1].astype(F32)
            direct[2, :, hi] = total.astype(BF16)
            self.last.append(send(direct.at[2, :, hi], fin.at[turn, 1, :, hi], z_bwd))

        def result(self):
            turn = self.turn
            self.core[0].wait_recv()
            mine = self.both(0, slice(0, D))
            arrived(self.last)
            return mine + fin[turn, 0].astype(F32) + fin[turn, 1].astype(F32)

    first_rows = Rows(0)

    def forward_pair(p):
        s0, s1 = slot(*PAIRS[p][0]), slot(*PAIRS[p][1])
        for ref, dense in ((slot_in, dense_in), (slot_out, dense_out)):
            both = jnp.concatenate([ref[s0].astype(F32), ref[s1].astype(F32)], axis=0)
            dense[p] = both.astype(BF16)
        pre = mm_nt(x[...].reshape(8 * R, D), dense_in[p])
        act, der = gelu_and_slope(pre)
        slope[p] = der.astype(BF16).reshape(4, 2 * R, 2 * U)
        act = act.astype(BF16)
        if p == 7:
            for dz in (2, 1, 3, 0):
                at = PLACE[dz]
                some = act[at * 2 * R:(at + 1) * 2 * R]
                for n in range(0, D, 256):
                    acc[at, :, n:n + 256] += mm(some, dense_out[p, :, n:n + 256])
                first_rows.offer(dz)
            return
        for n in range(0, D, 256):
            part = mm(act, dense_out[p, :, n:n + 256]).reshape(4, 2 * R, 256)
            if p == 0:
                acc[:, :, n:n + 256] = part
            else:
                acc[:, :, n:n + 256] += part

    for copy in locals_:
        copy.wait()
    for k in (3, 1):
        got("in", (k, 0))
        pass_on("in", (k, 0), "x")
        got("out", (0, k))
        pass_on("out", (0, k), "y")
    for k in (3, 1):
        give_both_ways("in", (k, 0), "y")
        give_both_ways("out", (0, k), "x")
    for k in (3, 1):
        got("in", (0, k))
        pass_on("in", (0, k), "y")
        got("out", (k, 0))
        pass_on("out", (k, 0), "x")
    arrived([x_up, x_down])
    sent([x_up, x_down])
    arrived(text_first)
    text_far = send(tall.at[0], tall.at[1], z_far)
    text_core = [send(tall.at[0], tall.at[2], core)]
    forward_pair(0)
    got_halves("in", (2, 0))
    give_both_ways("in", (2, 0), "y")
    got_halves("out", (0, 2))
    give_both_ways("out", (0, 2), "x")
    forward_pair(1)
    for j in (3, 1):
        for k in (3, 1):
            got("in", (j, k))
            pass_on("in", (j, k), "y")
            got("out", (k, j))
            pass_on("out", (k, j), "x")
    forward_pair(2)
    text_far.wait_recv()
    text_core.append(send(tall.at[1], tall.at[3], core))
    forward_pair(3)
    got_halves("in", (0, 2))
    got_halves("out", (2, 0))
    for k in (3, 1):
        got("in", (2, k))
        pass_on("in", (2, k), "y")
        got("out", (k, 2))
        pass_on("out", (k, 2), "x")
    forward_pair(4)
    got_halves("out", (2, 3))
    forward_pair(5)
    got_halves("out", (2, 1))
    got_halves("in", (3, 2))
    forward_pair(6)
    got_halves("in", (1, 2))
    got_halves("in", (2, 2))
    got_halves("out", (2, 2))
    forward_pair(7)

    rows = first_rows
    rows.far()
    rows.near_up()
    rows.near_down()
    rows.hops()
    mixed = rows.result()
    pooled_rows = pooled[pl.ds(pl.multiple_of(own_row, 16), R), :].astype(F32)
    resid_bf[...] = (pooled_rows + mixed).astype(BF16)

    own_cols = pl.ds(pl.multiple_of(z_lo * H, 128), H)
    other_cols = pl.ds(pl.multiple_of((1 - z_lo) * H, 128), H)
    rs[0, 0] = resid_bf[:, own_cols]
    rs_in = [
        send(resid_bf.at[:, other_cols], rs.at[0, PLACE[3]], z_fwd),
        send(resid_bf.at[:, other_cols], rs.at[0, PLACE[1]], z_bwd),
        send(resid_bf.at[:, own_cols], rs.at[0, PLACE[2]], z_far),
    ]

    project = mm(resid_bf[...], proj[...])
    inverse = lax.rsqrt(jnp.sum(project * project, axis=-1, keepdims=True) + 1e-06)
    unit_f = project * inverse
    embeds = unit_f.astype(BF16)
    eall[0, 0] = embeds

    arrived(text_core)
    scaling = scale[0]
    offset = bias[0]
    pairs = (R, 8 * R)
    same = lax.broadcasted_iota(jnp.int32, pairs, 0) == lax.broadcasted_iota(jnp.int32, pairs, 1)

    def other_side(mine, theirs, slabs, positive):
        total = None
        for q in range(0, slabs, 2):
            block = theirs[q:q + 2].reshape(8 * R, E)
            logits = scaling * mm_nt(mine, block) + offset
            soft = jax.nn.sigmoid(logits)
            if positive and q == 0:
                soft = jnp.where(same, -jax.nn.sigmoid(-logits), soft)
            term = mm(soft.astype(BF16), block)
            total = term if total is None else total + term
        return scaling * total

    grad_bf = x
    embed_grad = other_side(embeds, tall, 4, True)
    inner = jnp.sum(unit_f * embed_grad, axis=-1, keepdims=True)
    pd[0, 0] = (inverse * (embed_grad - unit_f * inner)).astype(BF16)
    pd_up = send(pd.at[0, 0], pd.at[0, PLACE[3]], z_fwd)
    pd_down = send(pd.at[0, 0], pd.at[0, PLACE[1]], z_bwd)
    pd_core = {0: send(pd.at[0, 0], pd.at[1, 0], core)}
    resid_grad[...] = mm_nt(pd[0, 0], proj[...])
    grad_bf[0, own, :] = resid_grad[...].astype(BF16)
    pd_core[0].wait_recv()
    grad_bf[0, other, :] = mm_nt(pd[1, 0], proj[...]).astype(BF16)

    def expand(first, last):
        both = pd[0:2, first:last]
        pieces = [both[j, n] for n in range(last - first) for j in range(2)]
        grads = mm_nt(jnp.concatenate(pieces, axis=0), proj[...])
        grad_bf[first:last] = grads.astype(BF16).reshape(last - first, 2 * R, D)

    def hidden_back(first, last):
        n = (last - first) * 2 * R
        for p in range(8):
            act_grad = mm_nt(grad_bf[first:last].reshape(n, D), dense_out[p])
            der = slope[p, first:last].reshape(n, 2 * U).astype(F32)
            slope[p, first:last] = (act_grad * der).astype(BF16).reshape(last - first, 2 * R, 2 * U)

    def input_back(dz):
        at = PLACE[dz]
        for n in range(0, D, 256):
            total = mm(slope[0, at], dense_in[0, :, n:n + 256])
            for p in range(1, 8):
                total = total + mm(slope[p, at], dense_in[p, :, n:n + 256])
            acc[at, :, n:n + 256] = total

    def pass_delta(dz):
        at = PLACE[dz]
        half, where = (pl.ds(0, E // 2), z_fwd) if dz == 3 else (pl.ds(E // 2, E // 2), z_bwd)
        on = send(pd.at[0, at, :, half], pd.at[0, PLACE[2], :, half], where)
        pd_core[dz] = send(pd.at[0, at], pd.at[1, at], core)
        return on

    hidden_back(0, 1)
    pd_up.wait_recv()
    pd_far = [pass_delta(3)]
    pd_down.wait_recv()
    pd_far.append(pass_delta(1))
    embeds_first = [send(eall.at[0, 0], eall.at[0, k], shifted(-k)) for k in (1, 2, 3)]
    arrived([pd_core[3], pd_core[1]])
    expand(1, 3)
    arrived(pd_far)
    pd_core[2] = send(pd.at[0, PLACE[2]], pd.at[1, PLACE[2]], core)
    arrived(rs_in)
    rs_core = send(rs.at[0], rs.at[1], core)
    hidden_back(1, 3)
    pd_core[2].wait_recv()
    expand(3, 4)
    hidden_back(3, 4)

    sent(list(rows.core.values()) + rows.last + [rows.up, rows.down])
    rows = Rows(1)
    input_back(2)
    rows.offer(2)
    rs_core.wait_recv()
    columns = pl.ds(pl.multiple_of(mp * 256, 128), 256)
    term = mm_tn(rs[...].reshape(8 * R, H), pd[:, :, :, columns].reshape(8 * R, 256))
    for n in range(16):
        pg[n % 4, n // 4] = term[n * 56:(n + 1) * 56, :].astype(BF16)
    pg_first = [send(pg.at[(xi + k) % 4], pg_in.at[k - 1], along_x[k]) for k in (1, 2, 3)]

    input_back(1)
    rows.offer(1)
    rows.far()
    input_back(3)
    rows.offer(3)
    rows.near_up()
    rows.near_down()
    rows.hops()
    arrived(embeds_first)
    embeds_core = send(eall.at[0], eall.at[1], core)
    input_back(0)
    rows.offer(0)
    embeds_core.wait_recv()
    unit_part[0] = other_side(tall[1, 0], eall, 2, False).astype(BF16)
    unit_far = send(unit_part.at[0], unit_part.at[1], z_far)

    arrived(pg_first)
    part = pg[xi].astype(F32)
    for k in range(3):
        part = part + pg_in[k].astype(F32)
    pg2[...] = part.astype(BF16)
    pg_second = [send(pg2.at[(yi + k) % 4], pg2_in.at[k - 1], along_y[k]) for k in (1, 2, 3)]

    tf, text_inv = text_parts()
    unit_grad = other_side(tall[0, 0], eall, 2, True)
    _, normed, inv_std = norm_rows(own_row)
    input_grad = rows.result()
    scaled = input_grad * gain[...].reshape(1, D)
    shift = scaled - jnp.mean(scaled, axis=-1, keepdims=True)
    shift = shift - normed * jnp.mean(scaled * normed, axis=-1, keepdims=True)
    d_pooled[...] = resid_grad[...] + inv_std * shift

    unit_far.wait_recv()
    unit_grad = unit_grad + unit_part[1].astype(F32)
    text_grad[...] = text_inv * (
        unit_grad - tf * jnp.sum(tf * unit_grad, axis=-1, keepdims=True)
    )

    arrived(pg_second)
    out = pg2[yi].astype(F32)
    for k in range(3):
        out = out + pg2_in[k].astype(F32)
    proj_grad[...] = out

    for copy in started:
        copy.wait_send()


def write_out(d_in, p_in, t_in, d_out, p_out, t_out):
    d_out[...] = d_in[...]
    p_out[...] = p_in[...]
    t_out[...] = t_in[...]


def per_device(pooled, ln_gain, w_in, w_out, proj, text, logit_scale, logit_bias):
    vmem = pl.BlockSpec(memory_space=pltpu.VMEM)
    smem = pl.BlockSpec(memory_space=pltpu.SMEM)
    hbm = pl.BlockSpec(memory_space=pl.ANY)
    results = pl.pallas_call(
        kernel,
        out_shape=(
            jax.ShapeDtypeStruct((R, D), F32),
            jax.ShapeDtypeStruct((56, 256), F32),
            jax.ShapeDtypeStruct((R, E), F32),
        ),
        in_specs=[vmem, vmem, hbm, hbm, hbm, vmem, smem, smem],
        out_specs=(vmem, vmem, vmem),
        scratch_shapes=[
            pltpu.VMEM((16, U, D), BF16),
            pltpu.VMEM((16, U, D), BF16),
            pltpu.VMEM((8, 2 * U, D), BF16),
            pltpu.VMEM((8, 2 * U, D), BF16),
            pltpu.VMEM((4, 2 * R, D), BF16),
            pltpu.VMEM((4, 2 * R, D), F32),
            pltpu.VMEM((8, 4, 2 * R, 2 * U), BF16),
            pltpu.VMEM((R, D), F32),
            pltpu.VMEM((4, 4, R, E), BF16),
            pltpu.VMEM((2, 4, R, E), BF16),
            pltpu.VMEM((D, E), BF16),
            pltpu.VMEM((4, R, D), BF16),
            pltpu.VMEM((2, 4, R, D), BF16),
            pltpu.VMEM((2, 2, R, H), BF16),
            pltpu.VMEM((2, 2, R, D), BF16),
            pltpu.VMEM((3, R, D), BF16),
            pltpu.VMEM((2, 4, R, E), BF16),
            pltpu.VMEM((R, D), BF16),
            pltpu.VMEM((2, 4, R, H), BF16),
            pltpu.VMEM((2, R, E), BF16),
            pltpu.VMEM((4, 4, 56, 256), BF16),
            pltpu.VMEM((3, 4, 56, 256), BF16),
            pltpu.VMEM((4, 56, 256), BF16),
            pltpu.VMEM((3, 56, 256), BF16),
            pltpu.SemaphoreType.DMA((N_SEMS,)),
            pltpu.SemaphoreType.DMA((N_SEMS,)),
            pltpu.SemaphoreType.DMA((3,)),
        ],
        compiler_params=pltpu.CompilerParams(
            collective_id=0, has_side_effects=True, vmem_limit_bytes=64 * 1024 * 1024
        ),
    )(pooled, ln_gain, w_in, w_out, proj, text, logit_scale, logit_bias)
    return pl.pallas_call(
        write_out,
        out_shape=[jax.ShapeDtypeStruct(r.shape, r.dtype) for r in results],
        in_specs=[vmem] * 3,
        out_specs=[vmem] * 3,
    )(*results)


def solution(mesh):
    in_specs = (
        P("dp", None),
        P(),
        P(("dp", "mp"), None),
        P(("dp", "mp"), None),
        P(),
        P(("dp", "mp"), None),
        P(),
        P(),
    )
    out_specs = (P(("dp", "mp"), None), P("dp", "mp"), P(("dp", "mp"), None))
    return jax.shard_map(
        per_device, mesh=mesh, in_specs=in_specs, out_specs=out_specs, check_vma=False
    )
```

```python
import functools

import jax
import jax.numpy as jnp
from jax import lax
from jax.experimental import pallas as pl
from jax.experimental.pallas import tpu as pltpu
from jax.sharding import PartitionSpec as P

D = 1792
H = D // 2
E = 1024
U = 120
R = 80
F32 = jnp.float32
BF16 = jnp.bfloat16
MESH = pl.DeviceIdType.MESH
PAIRS = (
    ((0, 0), (3, 0)),
    ((1, 0), (0, 3)),
    ((0, 1), (3, 3)),
    ((3, 1), (1, 3)),
    ((1, 1), (2, 0)),
    ((0, 2), (2, 3)),
    ((2, 1), (3, 2)),
    ((1, 2), (2, 2)),
)
PLACE = {0: 0, 1: 1, 3: 2, 2: 3}
N_SEMS = 128


def mm(a, b):
    return lax.dot_general(a, b, (((1,), (0,)), ((), ())), preferred_element_type=F32)


def mm_nt(a, b):
    return lax.dot_general(a, b, (((1,), (1,)), ((), ())), preferred_element_type=F32)


def mm_tn(a, b):
    return lax.dot_general(a, b, (((0,), (0,)), ((), ())), preferred_element_type=F32)


def gelu_and_slope(v):
    c = 0.7978845608028654
    v2 = v * v
    t = jnp.tanh(c * v * (1.0 + 0.044715 * v2))
    half = 0.5 * (1.0 + t)
    act = v * half
    slope = half + (0.5 * v) * (1.0 - t * t) * (c * (1.0 + 3.0 * 0.044715 * v2))
    return act, slope


def kernel(
    pooled, gain, w_in, w_out, proj_hbm, text, scale, bias,
    d_pooled, proj_grad, text_grad,
    slot_in, slot_out, dense_in, dense_out, x, acc, slope, resid_grad,
    tall, eall, proj, stage, core_in, hop, fin, direct, pd, resid_bf, rs, unit_part,
    pg, pg_in, pg2, pg2_in, send_sems, recv_sems, local_sems,
):
    dp = lax.axis_index("dp")
    mp = lax.axis_index("mp")
    z_lo = dp // 16
    yi = (dp // 4) % 4
    xi = dp % 4
    z_hi = mp // 2
    c = mp % 2
    z = z_hi * 2 + z_lo

    def place(dx=0, dy=0, dz=0, other=False):
        nz = (z + dz) % 4
        ndp = (nz % 2) * 16 + ((yi + dy) % 4) * 4 + (xi + dx) % 4
        nmp = (nz // 2) * 2 + (1 - c if other else c)
        return {"dp": ndp, "mp": nmp}

    def shifted(k):
        return {"dp": (dp + k + 32) % 32, "mp": mp}

    along_x = {k: place(dx=k) for k in (3, 1, 2)}
    along_y = {k: place(dy=k) for k in (3, 1, 2)}
    z_fwd, z_bwd, z_far = place(dz=1), place(dz=3), place(dz=2)
    core = place(other=True)

    count = [0]
    started = []

    def send(src, dst, where):
        n = count[0]
        count[0] += 1
        copy = pltpu.make_async_remote_copy(
            src_ref=src, dst_ref=dst, send_sem=send_sems.at[n], recv_sem=recv_sems.at[n],
            device_id=where, device_id_type=MESH,
        )
        copy.start()
        started.append(copy)
        return copy

    def sent(copies):
        for copy in copies:
            copy.wait_send()
            started[:] = [other for other in started if other is not copy]

    def arrived(copies):
        for copy in copies:
            copy.wait_recv()

    def slot(dx, dy):
        return dy * 4 + dx

    locals_ = [
        pltpu.make_async_copy(w_in, slot_in.at[0], local_sems.at[0]),
        pltpu.make_async_copy(w_out, slot_out.at[0], local_sems.at[1]),
        pltpu.make_async_copy(proj_hbm, proj, local_sems.at[2]),
    ]
    for copy in locals_:
        copy.start()

    peers = list(along_x.values()) + list(along_y.values()) + [z_fwd, z_bwd, z_far, core]
    peers += [shifted(k) for k in (-3, -2, -1, 1, 2, 3)]
    barrier = pltpu.get_barrier_semaphore()
    for peer in peers:
        pl.semaphore_signal(barrier, inc=1, device_id=peer, device_id_type=MESH)
    pl.semaphore_wait(barrier, len(peers))

    arrive = {}

    def give(which, src, at, where, half=None):
        target = (slot_in if which == "in" else slot_out).at[slot(*at)]
        if half is not None:
            columns = pl.ds(half * H, H)
            target, src = target.at[:, columns], src.at[:, columns]
        arrive[which, at, half] = send(src, target, where)

    def held(which, at):
        return (slot_in if which == "in" else slot_out).at[slot(*at)]

    def got(which, at, half=None):
        arrive[which, at, half].wait_recv()

    def got_halves(which, at):
        got(which, at, 0)
        got(which, at, 1)

    def give_both_ways(which, at, axis, src=None):
        src = held(which, at) if src is None else src
        if axis == "x":
            give(which, src, ((at[0] + 3) % 4, at[1]), along_x[1])
            give(which, src, ((at[0] + 1) % 4, at[1]), along_x[3])
        else:
            give(which, src, (at[0], (at[1] + 3) % 4), along_y[1])
            give(which, src, (at[0], (at[1] + 1) % 4), along_y[3])

    def pass_on(which, at, axis):
        dx, dy = at
        src = held(which, at)
        if axis == "x":
            k, half = (1, 0) if dx == 3 else (3, 1)
            give(which, src, (2, dy), along_x[k], half)
        else:
            k, half = (1, 0) if dy == 3 else (3, 1)
            give(which, src, (dx, 2), along_y[k], half)

    give_both_ways("in", (0, 0), "x", w_in)
    give_both_ways("out", (0, 0), "y", w_out)
    give_both_ways("out", (0, 0), "x", w_out)
    give_both_ways("in", (0, 0), "y", w_in)

    def norm_rows(start):
        h = pooled[pl.ds(pl.multiple_of(start, 16), R), :].astype(F32)
        center = h - jnp.mean(h, axis=-1, keepdims=True)
        inv_std = lax.rsqrt(jnp.mean(center * center, axis=-1, keepdims=True) + 1e-06)
        return h, center * inv_std, inv_std

    own_row = z_hi * 160 + c * R
    other_row = z_hi * 160 + (1 - c) * R
    far_own = (1 - z_hi) * 160 + c * R
    far_other = (1 - z_hi) * 160 + (1 - c) * R

    def fill_x(dz, j, start):
        x[PLACE[dz], j * R:(j + 1) * R, :] = (norm_rows(start)[1] * gain[...].reshape(1, D)).astype(BF16)

    fill_x(0, 0, own_row)
    fill_x(0, 1, other_row)
    x_up = send(x.at[PLACE[0]], x.at[PLACE[3]], z_fwd)
    x_down = send(x.at[PLACE[0]], x.at[PLACE[1]], z_bwd)

    def text_parts():
        t = text[...].astype(F32)
        inv = lax.rsqrt(jnp.sum(t * t, axis=-1, keepdims=True) + 1e-06)
        return t * inv, inv

    tall[0, 0] = text_parts()[0].astype(BF16)
    text_first = [send(tall.at[0, 0], tall.at[0, k], shifted(k)) for k in (1, 2, 3)]
    fill_x(2, 0, far_own)
    fill_x(2, 1, far_other)

    def forward_pair(p):
        s0, s1 = slot(*PAIRS[p][0]), slot(*PAIRS[p][1])
        for ref, dense in ((slot_in, dense_in), (slot_out, dense_out)):
            both = jnp.concatenate([ref[s0].astype(F32), ref[s1].astype(F32)], axis=0)
            dense[p] = both.astype(BF16)
        pre = mm_nt(x[...].reshape(8 * R, D), dense_in[p])
        act, der = gelu_and_slope(pre)
        slope[p] = der.astype(BF16).reshape(4, 2 * R, 2 * U)
        act = act.astype(BF16)
        for n in range(0, D, 256):
            part = mm(act, dense_out[p, :, n:n + 256]).reshape(4, 2 * R, 256)
            if p == 0:
                acc[:, :, n:n + 256] = part
            else:
                acc[:, :, n:n + 256] += part

    for copy in locals_:
        copy.wait()
    for k in (3, 1):
        got("in", (k, 0))
        pass_on("in", (k, 0), "x")
        got("out", (0, k))
        pass_on("out", (0, k), "y")
    for k in (3, 1):
        give_both_ways("in", (k, 0), "y")
        give_both_ways("out", (0, k), "x")
    for k in (3, 1):
        got("in", (0, k))
        pass_on("in", (0, k), "y")
        got("out", (k, 0))
        pass_on("out", (k, 0), "x")
    arrived([x_up, x_down])
    sent([x_up, x_down])
    arrived(text_first)
    text_far = send(tall.at[0], tall.at[1], z_far)
    text_core = [send(tall.at[0], tall.at[2], core)]
    forward_pair(0)
    got_halves("in", (2, 0))
    give_both_ways("in", (2, 0), "y")
    got_halves("out", (0, 2))
    give_both_ways("out", (0, 2), "x")
    forward_pair(1)
    for j in (3, 1):
        for k in (3, 1):
            got("in", (j, k))
            pass_on("in", (j, k), "y")
            got("out", (k, j))
            pass_on("out", (k, j), "x")
    forward_pair(2)
    text_far.wait_recv()
    text_core.append(send(tall.at[1], tall.at[3], core))
    forward_pair(3)
    got_halves("in", (0, 2))
    got_halves("out", (2, 0))
    for k in (3, 1):
        got("in", (2, k))
        pass_on("in", (2, k), "y")
        got("out", (k, 2))
        pass_on("out", (k, 2), "x")
    forward_pair(4)
    got_halves("out", (2, 3))
    forward_pair(5)
    got_halves("out", (2, 1))
    got_halves("in", (3, 2))
    forward_pair(6)
    got_halves("in", (1, 2))
    got_halves("in", (2, 2))
    got_halves("out", (2, 2))
    forward_pair(7)

    lo, hi = slice(0, H), slice(H, D)
    own, other = slice(0, R), slice(R, 2 * R)

    class Rows:
        def __init__(self, turn):
            self.turn = turn
            self.core = {}
            self.last = []

        def offer(self, dz):
            stage[dz] = acc[PLACE[dz], other, :].astype(BF16)
            self.core[dz] = send(stage.at[dz], core_in.at[self.turn, dz], core)

        def both(self, dz, columns):
            theirs = core_in[self.turn, dz, :, columns].astype(F32)
            return acc[PLACE[dz], own, columns] + theirs

        def far(self):
            turn = self.turn
            self.core[2].wait_recv()
            direct[0] = self.both(2, slice(0, D)).astype(BF16)
            self.up = send(direct.at[0, :, lo], hop.at[turn, 0], z_fwd)
            self.down = send(direct.at[0, :, hi], hop.at[turn, 1], z_bwd)

        def near_up(self):
            turn = self.turn
            self.core[1].wait_recv()
            direct[1, :, hi] = self.both(1, hi).astype(BF16)
            self.last.append(send(direct.at[1, :, hi], fin.at[turn, 0, :, hi], z_fwd))

        def near_down(self):
            turn = self.turn
            self.core[3].wait_recv()
            direct[2, :, lo] = self.both(3, lo).astype(BF16)
            self.last.append(send(direct.at[2, :, lo], fin.at[turn, 1, :, lo], z_bwd))

        def hops(self):
            turn = self.turn
            self.up.wait_recv()
            total = self.both(1, lo) + hop[turn, 0].astype(F32)
            direct[1, :, lo] = total.astype(BF16)
            self.last.append(send(direct.at[1, :, lo], fin.at[turn, 0, :, lo], z_fwd))
            self.down.wait_recv()
            total = self.both(3, hi) + hop[turn, 1].astype(F32)
            direct[2, :, hi] = total.astype(BF16)
            self.last.append(send(direct.at[2, :, hi], fin.at[turn, 1, :, hi], z_bwd))

        def result(self):
            turn = self.turn
            self.core[0].wait_recv()
            mine = self.both(0, slice(0, D))
            arrived(self.last)
            return mine + fin[turn, 0].astype(F32) + fin[turn, 1].astype(F32)

    rows = Rows(0)
    for dz in (2, 1, 3, 0):
        rows.offer(dz)
    rows.far()
    rows.near_up()
    rows.near_down()
    rows.hops()
    mixed = rows.result()
    pooled_rows = pooled[pl.ds(pl.multiple_of(own_row, 16), R), :].astype(F32)
    resid_bf[...] = (pooled_rows + mixed).astype(BF16)

    own_cols = pl.ds(pl.multiple_of(z_lo * H, 128), H)
    other_cols = pl.ds(pl.multiple_of((1 - z_lo) * H, 128), H)
    rs[0, 0] = resid_bf[:, own_cols]
    rs_in = [
        send(resid_bf.at[:, other_cols], rs.at[0, PLACE[3]], z_fwd),
        send(resid_bf.at[:, other_cols], rs.at[0, PLACE[1]], z_bwd),
        send(resid_bf.at[:, own_cols], rs.at[0, PLACE[2]], z_far),
    ]

    project = mm(resid_bf[...], proj[...])
    inverse = lax.rsqrt(jnp.sum(project * project, axis=-1, keepdims=True) + 1e-06)
    unit_f = project * inverse
    embeds = unit_f.astype(BF16)
    eall[0, 0] = embeds

    arrived(text_core)
    scaling = scale[0]
    offset = bias[0]
    pairs = (R, 8 * R)
    same = lax.broadcasted_iota(jnp.int32, pairs, 0) == lax.broadcasted_iota(jnp.int32, pairs, 1)

    def other_side(mine, theirs, slabs, positive):
        total = None
        for q in range(0, slabs, 2):
            block = theirs[q:q + 2].reshape(8 * R, E)
            logits = scaling * mm_nt(mine, block) + offset
            soft = jax.nn.sigmoid(logits)
            if positive and q == 0:
                soft = jnp.where(same, -jax.nn.sigmoid(-logits), soft)
            term = mm(soft.astype(BF16), block)
            total = term if total is None else total + term
        return scaling * total

    grad_bf = x
    embed_grad = other_side(embeds, tall, 4, True)
    inner = jnp.sum(unit_f * embed_grad, axis=-1, keepdims=True)
    pd[0, 0] = (inverse * (embed_grad - unit_f * inner)).astype(BF16)
    pd_up = send(pd.at[0, 0], pd.at[0, PLACE[3]], z_fwd)
    pd_down = send(pd.at[0, 0], pd.at[0, PLACE[1]], z_bwd)
    pd_core = {0: send(pd.at[0, 0], pd.at[1, 0], core)}
    resid_grad[...] = mm_nt(pd[0, 0], proj[...])
    grad_bf[0, own, :] = resid_grad[...].astype(BF16)
    pd_core[0].wait_recv()
    grad_bf[0, other, :] = mm_nt(pd[1, 0], proj[...]).astype(BF16)

    def expand(first, last):
        both = pd[0:2, first:last]
        pieces = [both[j, n] for n in range(last - first) for j in range(2)]
        grads = mm_nt(jnp.concatenate(pieces, axis=0), proj[...])
        grad_bf[first:last] = grads.astype(BF16).reshape(last - first, 2 * R, D)

    def hidden_back(first, last):
        n = (last - first) * 2 * R
        for p in range(8):
            act_grad = mm_nt(grad_bf[first:last].reshape(n, D), dense_out[p])
            der = slope[p, first:last].reshape(n, 2 * U).astype(F32)
            slope[p, first:last] = (act_grad * der).astype(BF16).reshape(last - first, 2 * R, 2 * U)

    def input_back(dz):
        at = PLACE[dz]
        for n in range(0, D, 256):
            total = mm(slope[0, at], dense_in[0, :, n:n + 256])
            for p in range(1, 8):
                total = total + mm(slope[p, at], dense_in[p, :, n:n + 256])
            acc[at, :, n:n + 256] = total

    def pass_delta(dz):
        at = PLACE[dz]
        half, where = (pl.ds(0, E // 2), z_fwd) if dz == 3 else (pl.ds(E // 2, E // 2), z_bwd)
        on = send(pd.at[0, at, :, half], pd.at[0, PLACE[2], :, half], where)
        pd_core[dz] = send(pd.at[0, at], pd.at[1, at], core)
        return on

    hidden_back(0, 1)
    pd_up.wait_recv()
    pd_far = [pass_delta(3)]
    pd_down.wait_recv()
    pd_far.append(pass_delta(1))
    embeds_first = [send(eall.at[0, 0], eall.at[0, k], shifted(-k)) for k in (1, 2, 3)]
    arrived([pd_core[3], pd_core[1]])
    expand(1, 3)
    arrived(pd_far)
    pd_core[2] = send(pd.at[0, PLACE[2]], pd.at[1, PLACE[2]], core)
    hidden_back(1, 3)
    pd_core[2].wait_recv()
    expand(3, 4)
    hidden_back(3, 4)

    sent(list(rows.core.values()) + rows.last + [rows.up, rows.down])
    rows = Rows(1)
    input_back(2)
    rows.offer(2)
    arrived(rs_in)
    rs_core = send(rs.at[0], rs.at[1], core)
    arrived(embeds_first)
    embeds_core = send(eall.at[0], eall.at[1], core)
    input_back(1)
    rows.offer(1)
    rows.far()
    input_back(3)
    rows.offer(3)
    rows.near_up()
    rows.near_down()

    rs_core.wait_recv()
    columns = pl.ds(pl.multiple_of(mp * 256, 128), 256)
    term = mm_tn(rs[...].reshape(8 * R, H), pd[:, :, :, columns].reshape(8 * R, 256))
    for n in range(16):
        pg[n % 4, n // 4] = term[n * 56:(n + 1) * 56, :].astype(BF16)
    pg_first = [send(pg.at[(xi + k) % 4], pg_in.at[k - 1], along_x[k]) for k in (1, 2, 3)]
    rows.hops()
    embeds_core.wait_recv()
    unit_part[0] = other_side(tall[1, 0], eall, 2, False).astype(BF16)
    unit_far = send(unit_part.at[0], unit_part.at[1], z_far)
    input_back(0)
    rows.offer(0)

    arrived(pg_first)
    part = pg[xi].astype(F32)
    for k in range(3):
        part = part + pg_in[k].astype(F32)
    pg2[...] = part.astype(BF16)
    pg_second = [send(pg2.at[(yi + k) % 4], pg2_in.at[k - 1], along_y[k]) for k in (1, 2, 3)]

    tf, text_inv = text_parts()
    unit_grad = other_side(tall[0, 0], eall, 2, True)
    _, normed, inv_std = norm_rows(own_row)
    input_grad = rows.result()
    scaled = input_grad * gain[...].reshape(1, D)
    shift = scaled - jnp.mean(scaled, axis=-1, keepdims=True)
    shift = shift - normed * jnp.mean(scaled * normed, axis=-1, keepdims=True)
    d_pooled[...] = resid_grad[...] + inv_std * shift

    unit_far.wait_recv()
    unit_grad = unit_grad + unit_part[1].astype(F32)
    text_grad[...] = text_inv * (
        unit_grad - tf * jnp.sum(tf * unit_grad, axis=-1, keepdims=True)
    )

    arrived(pg_second)
    out = pg2[yi].astype(F32)
    for k in range(3):
        out = out + pg2_in[k].astype(F32)
    proj_grad[...] = out

    for copy in started:
        copy.wait_send()


def write_out(d_in, p_in, t_in, d_out, p_out, t_out):
    d_out[...] = d_in[...]
    p_out[...] = p_in[...]
    t_out[...] = t_in[...]


def per_device(pooled, ln_gain, w_in, w_out, proj, text, logit_scale, logit_bias):
    vmem = pl.BlockSpec(memory_space=pltpu.VMEM)
    smem = pl.BlockSpec(memory_space=pltpu.SMEM)
    hbm = pl.BlockSpec(memory_space=pl.ANY)
    results = pl.pallas_call(
        kernel,
        out_shape=(
            jax.ShapeDtypeStruct((R, D), F32),
            jax.ShapeDtypeStruct((56, 256), F32),
            jax.ShapeDtypeStruct((R, E), F32),
        ),
        in_specs=[vmem, vmem, hbm, hbm, hbm, vmem, smem, smem],
        out_specs=(vmem, vmem, vmem),
        scratch_shapes=[
            pltpu.VMEM((16, U, D), BF16),
            pltpu.VMEM((16, U, D), BF16),
            pltpu.VMEM((8, 2 * U, D), BF16),
            pltpu.VMEM((8, 2 * U, D), BF16),
            pltpu.VMEM((4, 2 * R, D), BF16),
            pltpu.VMEM((4, 2 * R, D), F32),
            pltpu.VMEM((8, 4, 2 * R, 2 * U), BF16),
            pltpu.VMEM((R, D), F32),
            pltpu.VMEM((4, 4, R, E), BF16),
            pltpu.VMEM((2, 4, R, E), BF16),
            pltpu.VMEM((D, E), BF16),
            pltpu.VMEM((4, R, D), BF16),
            pltpu.VMEM((2, 4, R, D), BF16),
            pltpu.VMEM((2, 2, R, H), BF16),
            pltpu.VMEM((2, 2, R, D), BF16),
            pltpu.VMEM((3, R, D), BF16),
            pltpu.VMEM((2, 4, R, E), BF16),
            pltpu.VMEM((R, D), BF16),
            pltpu.VMEM((2, 4, R, H), BF16),
            pltpu.VMEM((2, R, E), BF16),
            pltpu.VMEM((4, 4, 56, 256), BF16),
            pltpu.VMEM((3, 4, 56, 256), BF16),
            pltpu.VMEM((4, 56, 256), BF16),
            pltpu.VMEM((3, 56, 256), BF16),
            pltpu.SemaphoreType.DMA((N_SEMS,)),
            pltpu.SemaphoreType.DMA((N_SEMS,)),
            pltpu.SemaphoreType.DMA((3,)),
        ],
        compiler_params=pltpu.CompilerParams(
            collective_id=0, has_side_effects=True, vmem_limit_bytes=64 * 1024 * 1024
        ),
    )(pooled, ln_gain, w_in, w_out, proj, text, logit_scale, logit_bias)
    return pl.pallas_call(
        write_out,
        out_shape=[jax.ShapeDtypeStruct(r.shape, r.dtype) for r in results],
        in_specs=[vmem] * 3,
        out_specs=[vmem] * 3,
    )(*results)


def solution(mesh):
    in_specs = (
        P("dp", None),
        P(),
        P(("dp", "mp"), None),
        P(("dp", "mp"), None),
        P(),
        P(("dp", "mp"), None),
        P(),
        P(),
    )
    out_specs = (P(("dp", "mp"), None), P("dp", "mp"), P(("dp", "mp"), None))
    return jax.shard_map(
        per_device, mesh=mesh, in_specs=in_specs, out_specs=out_specs, check_vma=False
    )
```

```python
import functools

import jax
import jax.numpy as jnp
from jax import lax
from jax.experimental import pallas as pl
from jax.experimental.pallas import tpu as pltpu
from jax.sharding import PartitionSpec as P

D = 1792
H = D // 2
E = 1024
U = 120
R = 80
F32 = jnp.float32
BF16 = jnp.bfloat16
MESH = pl.DeviceIdType.MESH
PAIRS = (
    ((0, 0), (3, 0)),
    ((1, 0), (0, 3)),
    ((0, 1), (3, 3)),
    ((3, 1), (1, 3)),
    ((1, 1), (2, 0)),
    ((0, 2), (2, 3)),
    ((2, 1), (3, 2)),
    ((1, 2), (2, 2)),
)
PLACE = {0: 0, 1: 1, 3: 2, 2: 3}
N_SEMS = 128


def mm(a, b):
    return lax.dot_general(a, b, (((1,), (0,)), ((), ())), preferred_element_type=F32)


def mm_nt(a, b):
    return lax.dot_general(a, b, (((1,), (1,)), ((), ())), preferred_element_type=F32)


def mm_tn(a, b):
    return lax.dot_general(a, b, (((0,), (0,)), ((), ())), preferred_element_type=F32)


def gelu_and_slope(v):
    c = 0.7978845608028654
    v2 = v * v
    t = jnp.tanh(c * v * (1.0 + 0.044715 * v2))
    half = 0.5 * (1.0 + t)
    act = v * half
    slope = half + (0.5 * v) * (1.0 - t * t) * (c * (1.0 + 3.0 * 0.044715 * v2))
    return act, slope


def kernel(
    pooled, gain, w_in, w_out, proj_hbm, text, scale, bias,
    d_pooled, proj_grad, text_grad,
    slot_in, slot_out, dense_in, dense_out, x, acc, slope, resid_grad,
    tall, eall, proj, stage, core_in, hop, fin, direct, pd, resid_bf, rs, unit_part,
    pg, pg_in, pg2, pg2_in, send_sems, recv_sems, local_sems,
):
    dp = lax.axis_index("dp")
    mp = lax.axis_index("mp")
    z_lo = dp // 16
    yi = (dp // 4) % 4
    xi = dp % 4
    z_hi = mp // 2
    c = mp % 2
    z = z_hi * 2 + z_lo

    def place(dx=0, dy=0, dz=0, other=False):
        nz = (z + dz) % 4
        ndp = (nz % 2) * 16 + ((yi + dy) % 4) * 4 + (xi + dx) % 4
        nmp = (nz // 2) * 2 + (1 - c if other else c)
        return {"dp": ndp, "mp": nmp}

    def shifted(k):
        return {"dp": (dp + k + 32) % 32, "mp": mp}

    along_x = {k: place(dx=k) for k in (3, 1, 2)}
    along_y = {k: place(dy=k) for k in (3, 1, 2)}
    z_fwd, z_bwd, z_far = place(dz=1), place(dz=3), place(dz=2)
    core = place(other=True)

    count = [0]
    started = []

    def send(src, dst, where):
        n = count[0]
        count[0] += 1
        copy = pltpu.make_async_remote_copy(
            src_ref=src, dst_ref=dst, send_sem=send_sems.at[n], recv_sem=recv_sems.at[n],
            device_id=where, device_id_type=MESH,
        )
        copy.start()
        started.append(copy)
        return copy

    def sent(copies):
        for copy in copies:
            copy.wait_send()
            started[:] = [other for other in started if other is not copy]

    def arrived(copies):
        for copy in copies:
            copy.wait_recv()

    def slot(dx, dy):
        return dy * 4 + dx

    locals_ = [
        pltpu.make_async_copy(w_in, slot_in.at[0], local_sems.at[0]),
        pltpu.make_async_copy(w_out, slot_out.at[0], local_sems.at[1]),
        pltpu.make_async_copy(proj_hbm, proj, local_sems.at[2]),
    ]
    for copy in locals_:
        copy.start()

    peers = list(along_x.values()) + list(along_y.values()) + [z_fwd, z_bwd, z_far, core]
    peers += [shifted(k) for k in (-3, -2, -1, 1, 2, 3)]
    barrier = pltpu.get_barrier_semaphore()
    for peer in peers:
        pl.semaphore_signal(barrier, inc=1, device_id=peer, device_id_type=MESH)
    pl.semaphore_wait(barrier, len(peers))

    arrive = {}

    def give(which, src, at, where, half=None):
        target = (slot_in if which == "in" else slot_out).at[slot(*at)]
        if half is not None:
            columns = pl.ds(half * H, H)
            target, src = target.at[:, columns], src.at[:, columns]
        arrive[which, at, half] = send(src, target, where)

    def held(which, at):
        return (slot_in if which == "in" else slot_out).at[slot(*at)]

    def got(which, at, half=None):
        arrive[which, at, half].wait_recv()

    def got_halves(which, at):
        got(which, at, 0)
        got(which, at, 1)

    def give_both_ways(which, at, axis, src=None):
        src = held(which, at) if src is None else src
        if axis == "x":
            give(which, src, ((at[0] + 3) % 4, at[1]), along_x[1])
            give(which, src, ((at[0] + 1) % 4, at[1]), along_x[3])
        else:
            give(which, src, (at[0], (at[1] + 3) % 4), along_y[1])
            give(which, src, (at[0], (at[1] + 1) % 4), along_y[3])

    def pass_on(which, at, axis):
        dx, dy = at
        src = held(which, at)
        if axis == "x":
            k, half = (1, 0) if dx == 3 else (3, 1)
            give(which, src, (2, dy), along_x[k], half)
        else:
            k, half = (1, 0) if dy == 3 else (3, 1)
            give(which, src, (dx, 2), along_y[k], half)

    give_both_ways("in", (0, 0), "x", w_in)
    give_both_ways("out", (0, 0), "y", w_out)
    give_both_ways("out", (0, 0), "x", w_out)
    give_both_ways("in", (0, 0), "y", w_in)

    def norm_rows(start):
        h = pooled[pl.ds(pl.multiple_of(start, 16), R), :].astype(F32)
        center = h - jnp.mean(h, axis=-1, keepdims=True)
        inv_std = lax.rsqrt(jnp.mean(center * center, axis=-1, keepdims=True) + 1e-06)
        return h, center * inv_std, inv_std

    own_row = z_hi * 160 + c * R
    other_row = z_hi * 160 + (1 - c) * R
    far_own = (1 - z_hi) * 160 + c * R
    far_other = (1 - z_hi) * 160 + (1 - c) * R

    def fill_x(dz, j, start):
        x[PLACE[dz], j * R:(j + 1) * R, :] = (norm_rows(start)[1] * gain[...].reshape(1, D)).astype(BF16)

    fill_x(0, 0, own_row)
    fill_x(0, 1, other_row)
    x_up = send(x.at[PLACE[0]], x.at[PLACE[3]], z_fwd)
    x_down = send(x.at[PLACE[0]], x.at[PLACE[1]], z_bwd)

    def text_parts():
        t = text[...].astype(F32)
        inv = lax.rsqrt(jnp.sum(t * t, axis=-1, keepdims=True) + 1e-06)
        return t * inv, inv

    tall[0, 0] = text_parts()[0].astype(BF16)
    text_first = [send(tall.at[0, 0], tall.at[0, k], shifted(k)) for k in (1, 2, 3)]
    fill_x(2, 0, far_own)
    fill_x(2, 1, far_other)

    def forward_pair(p):
        s0, s1 = slot(*PAIRS[p][0]), slot(*PAIRS[p][1])
        for ref, dense in ((slot_in, dense_in), (slot_out, dense_out)):
            both = jnp.concatenate([ref[s0].astype(F32), ref[s1].astype(F32)], axis=0)
            dense[p] = both.astype(BF16)
        pre = mm_nt(x[...].reshape(8 * R, D), dense_in[p])
        act, der = gelu_and_slope(pre)
        slope[p] = der.astype(BF16).reshape(4, 2 * R, 2 * U)
        act = act.astype(BF16)
        for n in range(0, D, 256):
            part = mm(act, dense_out[p, :, n:n + 256]).reshape(4, 2 * R, 256)
            if p == 0:
                acc[:, :, n:n + 256] = part
            else:
                acc[:, :, n:n + 256] += part

    for copy in locals_:
        copy.wait()
    for k in (3, 1):
        got("in", (k, 0))
        pass_on("in", (k, 0), "x")
        got("out", (0, k))
        pass_on("out", (0, k), "y")
    for k in (3, 1):
        give_both_ways("in", (k, 0), "y")
        give_both_ways("out", (0, k), "x")
    for k in (3, 1):
        got("in", (0, k))
        pass_on("in", (0, k), "y")
        got("out", (k, 0))
        pass_on("out", (k, 0), "x")
    arrived([x_up, x_down])
    sent([x_up, x_down])
    arrived(text_first)
    text_far = send(tall.at[0], tall.at[1], z_far)
    text_core = [send(tall.at[0], tall.at[2], core)]
    forward_pair(0)
    got_halves("in", (2, 0))
    give_both_ways("in", (2, 0), "y")
    got_halves("out", (0, 2))
    give_both_ways("out", (0, 2), "x")
    forward_pair(1)
    for j in (3, 1):
        for k in (3, 1):
            got("in", (j, k))
            pass_on("in", (j, k), "y")
            got("out", (k, j))
            pass_on("out", (k, j), "x")
    forward_pair(2)
    text_far.wait_recv()
    text_core.append(send(tall.at[1], tall.at[3], core))
    forward_pair(3)
    got_halves("in", (0, 2))
    got_halves("out", (2, 0))
    for k in (3, 1):
        got("in", (2, k))
        pass_on("in", (2, k), "y")
        got("out", (k, 2))
        pass_on("out", (k, 2), "x")
    forward_pair(4)
    got_halves("out", (2, 3))
    forward_pair(5)
    got_halves("out", (2, 1))
    got_halves("in", (3, 2))
    forward_pair(6)
    got_halves("in", (1, 2))
    got_halves("in", (2, 2))
    got_halves("out", (2, 2))
    forward_pair(7)

    lo, hi = slice(0, H), slice(H, D)
    own, other = slice(0, R), slice(R, 2 * R)

    class Rows:
        def __init__(self, turn):
            self.turn = turn
            self.core = {}
            self.last = []

        def offer(self, dz):
            stage[dz] = acc[PLACE[dz], other, :].astype(BF16)
            self.core[dz] = send(stage.at[dz], core_in.at[self.turn, dz], core)

        def both(self, dz, columns):
            theirs = core_in[self.turn, dz, :, columns].astype(F32)
            return acc[PLACE[dz], own, columns] + theirs

        def far(self):
            turn = self.turn
            self.core[2].wait_recv()
            direct[0] = self.both(2, slice(0, D)).astype(BF16)
            self.up = send(direct.at[0, :, lo], hop.at[turn, 0], z_fwd)
            self.down = send(direct.at[0, :, hi], hop.at[turn, 1], z_bwd)

        def near_up(self):
            turn = self.turn
            self.core[1].wait_recv()
            direct[1, :, hi] = self.both(1, hi).astype(BF16)
            self.last.append(send(direct.at[1, :, hi], fin.at[turn, 0, :, hi], z_fwd))

        def near_down(self):
            turn = self.turn
            self.core[3].wait_recv()
            direct[2, :, lo] = self.both(3, lo).astype(BF16)
            self.last.append(send(direct.at[2, :, lo], fin.at[turn, 1, :, lo], z_bwd))

        def hops(self):
            turn = self.turn
            self.up.wait_recv()
            total = self.both(1, lo) + hop[turn, 0].astype(F32)
            direct[1, :, lo] = total.astype(BF16)
            self.last.append(send(direct.at[1, :, lo], fin.at[turn, 0, :, lo], z_fwd))
            self.down.wait_recv()
            total = self.both(3, hi) + hop[turn, 1].astype(F32)
            direct[2, :, hi] = total.astype(BF16)
            self.last.append(send(direct.at[2, :, hi], fin.at[turn, 1, :, hi], z_bwd))

        def result(self):
            turn = self.turn
            self.core[0].wait_recv()
            mine = self.both(0, slice(0, D))
            arrived(self.last)
            return mine + fin[turn, 0].astype(F32) + fin[turn, 1].astype(F32)

    rows = Rows(0)
    for dz in (2, 1, 3, 0):
        rows.offer(dz)
    rows.far()
    rows.near_up()
    rows.near_down()
    rows.hops()
    mixed = rows.result()
    pooled_rows = pooled[pl.ds(pl.multiple_of(own_row, 16), R), :].astype(F32)
    resid_bf[...] = (pooled_rows + mixed).astype(BF16)

    own_cols = pl.ds(pl.multiple_of(z_lo * H, 128), H)
    other_cols = pl.ds(pl.multiple_of((1 - z_lo) * H, 128), H)
    rs[0, 0] = resid_bf[:, own_cols]
    rs_in = [
        send(resid_bf.at[:, other_cols], rs.at[0, PLACE[3]], z_fwd),
        send(resid_bf.at[:, other_cols], rs.at[0, PLACE[1]], z_bwd),
        send(resid_bf.at[:, own_cols], rs.at[0, PLACE[2]], z_far),
    ]

    project = mm(resid_bf[...], proj[...])
    inverse = lax.rsqrt(jnp.sum(project * project, axis=-1, keepdims=True) + 1e-06)
    unit_f = project * inverse
    embeds = unit_f.astype(BF16)
    eall[0, 0] = embeds

    arrived(text_core)
    scaling = scale[0]
    offset = bias[0]
    pairs = (R, 8 * R)
    same = lax.broadcasted_iota(jnp.int32, pairs, 0) == lax.broadcasted_iota(jnp.int32, pairs, 1)

    def other_side(mine, theirs, slabs, positive):
        total = None
        for q in range(0, slabs, 2):
            block = theirs[q:q + 2].reshape(8 * R, E)
            logits = scaling * mm_nt(mine, block) + offset
            soft = jax.nn.sigmoid(logits)
            if positive and q == 0:
                soft = jnp.where(same, -jax.nn.sigmoid(-logits), soft)
            term = mm(soft.astype(BF16), block)
            total = term if total is None else total + term
        return scaling * total

    grad_bf = x
    embed_grad = other_side(embeds, tall, 4, True)
    inner = jnp.sum(unit_f * embed_grad, axis=-1, keepdims=True)
    pd[0, 0] = (inverse * (embed_grad - unit_f * inner)).astype(BF16)
    pd_up = send(pd.at[0, 0], pd.at[0, PLACE[3]], z_fwd)
    pd_down = send(pd.at[0, 0], pd.at[0, PLACE[1]], z_bwd)
    pd_core = {0: send(pd.at[0, 0], pd.at[1, 0], core)}
    resid_grad[...] = mm_nt(pd[0, 0], proj[...])
    grad_bf[0, own, :] = resid_grad[...].astype(BF16)
    pd_core[0].wait_recv()
    grad_bf[0, other, :] = mm_nt(pd[1, 0], proj[...]).astype(BF16)

    def expand(first, last):
        both = pd[0:2, first:last]
        pieces = [both[j, n] for n in range(last - first) for j in range(2)]
        grads = mm_nt(jnp.concatenate(pieces, axis=0), proj[...])
        grad_bf[first:last] = grads.astype(BF16).reshape(last - first, 2 * R, D)

    def hidden_back(first, last):
        n = (last - first) * 2 * R
        for p in range(8):
            act_grad = mm_nt(grad_bf[first:last].reshape(n, D), dense_out[p])
            der = slope[p, first:last].reshape(n, 2 * U).astype(F32)
            slope[p, first:last] = (act_grad * der).astype(BF16).reshape(last - first, 2 * R, 2 * U)

    def input_back(dz):
        at = PLACE[dz]
        for n in range(0, D, 256):
            total = mm(slope[0, at], dense_in[0, :, n:n + 256])
            for p in range(1, 8):
                total = total + mm(slope[p, at], dense_in[p, :, n:n + 256])
            acc[at, :, n:n + 256] = total

    def pass_delta(dz):
        at = PLACE[dz]
        half, where = (pl.ds(0, E // 2), z_fwd) if dz == 3 else (pl.ds(E // 2, E // 2), z_bwd)
        on = send(pd.at[0, at, :, half], pd.at[0, PLACE[2], :, half], where)
        pd_core[dz] = send(pd.at[0, at], pd.at[1, at], core)
        return on

    hidden_back(0, 1)
    pd_up.wait_recv()
    pd_far = [pass_delta(3)]
    pd_down.wait_recv()
    pd_far.append(pass_delta(1))
    embeds_first = [send(eall.at[0, 0], eall.at[0, k], shifted(-k)) for k in (1, 2, 3)]
    arrived([pd_core[3], pd_core[1]])
    expand(1, 3)
    arrived(pd_far)
    pd_core[2] = send(pd.at[0, PLACE[2]], pd.at[1, PLACE[2]], core)
    hidden_back(1, 3)
    pd_core[2].wait_recv()
    expand(3, 4)
    hidden_back(3, 4)

    sent(list(rows.core.values()) + rows.last + [rows.up, rows.down])
    rows = Rows(1)
    input_back(2)
    rows.offer(2)
    arrived(rs_in)
    rs_core = send(rs.at[0], rs.at[1], core)
    input_back(1)
    rows.offer(1)
    rows.far()
    input_back(3)
    rows.offer(3)
    rows.near_up()
    rows.near_down()

    rs_core.wait_recv()
    columns = pl.ds(pl.multiple_of(mp * 256, 128), 256)
    term = mm_tn(rs[...].reshape(8 * R, H), pd[:, :, :, columns].reshape(8 * R, 256))
    for n in range(16):
        pg[n % 4, n // 4] = term[n * 56:(n + 1) * 56, :].astype(BF16)
    pg_first = [send(pg.at[(xi + k) % 4], pg_in.at[k - 1], along_x[k]) for k in (1, 2, 3)]
    rows.hops()
    arrived(embeds_first)
    embeds_core = send(eall.at[0], eall.at[1], core)
    input_back(0)
    rows.offer(0)
    embeds_core.wait_recv()
    unit_part[0] = other_side(tall[1, 0], eall, 2, False).astype(BF16)
    unit_far = send(unit_part.at[0], unit_part.at[1], z_far)

    arrived(pg_first)
    part = pg[xi].astype(F32)
    for k in range(3):
        part = part + pg_in[k].astype(F32)
    pg2[...] = part.astype(BF16)
    pg_second = [send(pg2.at[(yi + k) % 4], pg2_in.at[k - 1], along_y[k]) for k in (1, 2, 3)]

    tf, text_inv = text_parts()
    unit_grad = other_side(tall[0, 0], eall, 2, True)
    _, normed, inv_std = norm_rows(own_row)
    input_grad = rows.result()
    scaled = input_grad * gain[...].reshape(1, D)
    shift = scaled - jnp.mean(scaled, axis=-1, keepdims=True)
    shift = shift - normed * jnp.mean(scaled * normed, axis=-1, keepdims=True)
    d_pooled[...] = resid_grad[...] + inv_std * shift

    unit_far.wait_recv()
    unit_grad = unit_grad + unit_part[1].astype(F32)
    text_grad[...] = text_inv * (
        unit_grad - tf * jnp.sum(tf * unit_grad, axis=-1, keepdims=True)
    )

    arrived(pg_second)
    out = pg2[yi].astype(F32)
    for k in range(3):
        out = out + pg2_in[k].astype(F32)
    proj_grad[...] = out

    for copy in started:
        copy.wait_send()


def write_out(d_in, p_in, t_in, d_out, p_out, t_out):
    d_out[...] = d_in[...]
    p_out[...] = p_in[...]
    t_out[...] = t_in[...]


def per_device(pooled, ln_gain, w_in, w_out, proj, text, logit_scale, logit_bias):
    vmem = pl.BlockSpec(memory_space=pltpu.VMEM)
    smem = pl.BlockSpec(memory_space=pltpu.SMEM)
    hbm = pl.BlockSpec(memory_space=pl.ANY)
    results = pl.pallas_call(
        kernel,
        out_shape=(
            jax.ShapeDtypeStruct((R, D), F32),
            jax.ShapeDtypeStruct((56, 256), F32),
            jax.ShapeDtypeStruct((R, E), F32),
        ),
        in_specs=[vmem, vmem, hbm, hbm, hbm, vmem, smem, smem],
        out_specs=(vmem, vmem, vmem),
        scratch_shapes=[
            pltpu.VMEM((16, U, D), BF16),
            pltpu.VMEM((16, U, D), BF16),
            pltpu.VMEM((8, 2 * U, D), BF16),
            pltpu.VMEM((8, 2 * U, D), BF16),
            pltpu.VMEM((4, 2 * R, D), BF16),
            pltpu.VMEM((4, 2 * R, D), F32),
            pltpu.VMEM((8, 4, 2 * R, 2 * U), BF16),
            pltpu.VMEM((R, D), F32),
            pltpu.VMEM((4, 4, R, E), BF16),
            pltpu.VMEM((2, 4, R, E), BF16),
            pltpu.VMEM((D, E), BF16),
            pltpu.VMEM((4, R, D), BF16),
            pltpu.VMEM((2, 4, R, D), BF16),
            pltpu.VMEM((2, 2, R, H), BF16),
            pltpu.VMEM((2, 2, R, D), BF16),
            pltpu.VMEM((3, R, D), BF16),
            pltpu.VMEM((2, 4, R, E), BF16),
            pltpu.VMEM((R, D), BF16),
            pltpu.VMEM((2, 4, R, H), BF16),
            pltpu.VMEM((2, R, E), BF16),
            pltpu.VMEM((4, 4, 56, 256), BF16),
            pltpu.VMEM((3, 4, 56, 256), BF16),
            pltpu.VMEM((4, 56, 256), BF16),
            pltpu.VMEM((3, 56, 256), BF16),
            pltpu.SemaphoreType.DMA((N_SEMS,)),
            pltpu.SemaphoreType.DMA((N_SEMS,)),
            pltpu.SemaphoreType.DMA((3,)),
        ],
        compiler_params=pltpu.CompilerParams(
            collective_id=0, has_side_effects=True, vmem_limit_bytes=64 * 1024 * 1024
        ),
    )(pooled, ln_gain, w_in, w_out, proj, text, logit_scale, logit_bias)
    return pl.pallas_call(
        write_out,
        out_shape=[jax.ShapeDtypeStruct(r.shape, r.dtype) for r in results],
        in_specs=[vmem] * 3,
        out_specs=[vmem] * 3,
    )(*results)


def solution(mesh):
    in_specs = (
        P("dp", None),
        P(),
        P(("dp", "mp"), None),
        P(("dp", "mp"), None),
        P(),
        P(("dp", "mp"), None),
        P(),
        P(),
    )
    out_specs = (P(("dp", "mp"), None), P("dp", "mp"), P(("dp", "mp"), None))
    return jax.shard_map(
        per_device, mesh=mesh, in_specs=in_specs, out_specs=out_specs, check_vma=False
    )
```
